32 devices in a mesh: dp: 16 (over z, y, core), mp: 2 (over x).
Axes of the slice: x: 2, y: 2, z: 4, core: 2. Of those that a mesh axis runs over, the one named last changes fastest.
Arguments:
- patches: bfloat16 [32, 256, 1152], P('dp'), may hold values from -8 to 8
- time_bins: int32 [32], P('dp'), may hold values from 0 to 999
- class_ids: int32 [32], P('dp'), may hold values from 0 to 1000
- encoder_feats: bfloat16 [32, 256, 768], P('dp'), may hold values from -6 to 6
- cotangent: bfloat16 [32, 256, 1152], P('dp'), may hold values from -2 to 2
- w_qkv: bfloat16 [3, 1152, 1152], P(None, 'dp', 'mp'), may hold values from -0.1875 to 0.1875
- w_out: bfloat16 [1152, 1152], P('mp', 'dp'), may hold values from -0.75 to 0.75
- w_up: bfloat16 [1152, 4608], P('dp', 'mp'), may hold values from -0.1875 to 0.1875
- w_down: bfloat16 [4608, 1152], P('mp', 'dp'), may hold values from -0.09375 to 0.09375
- w_ada: bfloat16 [6, 1152, 1152], P(None, 'dp'), may hold values from -0.1875 to 0.1875
- time_table: bfloat16 [1000, 1152], P(None, 'dp'), may hold values from -4 to 4
- class_table: bfloat16 [1001, 1152], P(None, 'dp'), may hold values from -4 to 4
- inner_bias: float32 [2, 3456], P('mp', 'dp'), may hold values from -1.75 to 1.75
- b_out: float32 [1152], P('dp'), may hold values from -1.75 to 1.75
- b_down: float32 [1152], P('dp'), may hold values from -1.75 to 1.75
- b_ada: float32 [6, 1152], P(None, 'dp'), may hold values from -1.75 to 1.75
- w_first: bfloat16 [1152, 2048], P(None, ('dp', 'mp')), may hold values from -0.1875 to 0.1875
- w_second: bfloat16 [2048, 2048], P(None, ('dp', 'mp')), may hold values from -0.125 to 0.125
- w_third: bfloat16 [2048, 768], P(None, ('dp', 'mp')), may hold values from -0.125 to 0.125
- b_first: float32 [2048], P(('dp', 'mp')), may hold values from -1.75 to 1.75
- b_second: float32 [2048], P(('dp', 'mp')), may hold values from -1.75 to 1.75
- b_third: float32 [768], P(('dp', 'mp')), may hold values from -3 to 3
Outputs:
- block_out: bfloat16 [32, 256, 1152], P('dp')
- grad_patches: float32 [32, 256, 1152], P('dp')
- grad_qkv: float32 [3, 1152, 1152], P(None, 'dp', 'mp')
- grad_wout: float32 [1152, 1152], P('mp', 'dp')
- grad_wup: float32 [1152, 4608], P('dp', 'mp')
- grad_wdown: float32 [4608, 1152], P('mp', 'dp')
- grad_wada: float32 [6, 1152, 1152], P(None, 'dp')
- grad_time: float32 [1000, 1152], P(None, 'dp')
- grad_class: float32 [1001, 1152], P(None, 'dp')
- grad_inner: float32 [2, 3456], P('mp', 'dp')
- grad_bout: float32 [1152], P('dp')
- grad_bdown: float32 [1152], P('dp')
- grad_bada: float32 [6, 1152], P(None, 'dp')
- grad_wfirst: float32 [1152, 2048], P(None, ('dp', 'mp'))
- grad_wsecond: float32 [2048, 2048], P(None, ('dp', 'mp'))
- grad_wthird: float32 [2048, 768], P(None, ('dp', 'mp'))
- grad_bfirst: float32 [2048], P(('dp', 'mp'))
- grad_bsecond: float32 [2048], P(('dp', 'mp'))
- grad_bthird: float32 [768], P(('dp', 'mp'))
The draws below stay inside these ranges and needn't reach their ends.
All inputs are finite; a program needn't handle non-finite values.
Results may differ from the reference program's by a relative error of at most 0.04.
Values may be sent and summed in bfloat16 or wider, within the bound.
No kernel may reach another device: no remote copies, remote signals or barrier semaphores. Data moves between devices by JAX's collectives and lax.ppermute only.
A program may use at most 320 MiB of HBM per device.

```python
import math
import jax
import jax.numpy as jnp
import numpy as np
from jax import lax

D = 1152
HD = 72
FF = 4608
P_SIZE = 2048
E = 768
BINS = 1000
CLASSES = 1001
L = 256
IMAGES = 32
N_MP = 2


def with_ends(result, rng, least, largest):
    longest = result.shape.index(max(result.shape))
    spots = []
    for shift in (0, 1):
        where = [jax.random.randint(jax.random.fold_in(rng, axis), (), 0, length) for axis, length in enumerate(result.shape)]
        where[longest] = (where[longest] + shift) % result.shape[longest]
        spots.append(tuple(where))
    return result.at[spots[0]].set(least).at[spots[1]].set(largest)


def strengthened(drawn, key, source, target, shards_of, factor):
    def block_of(position):
        return (jnp.arange(drawn.shape[position]) // (drawn.shape[position] // shards_of)).reshape((-1,) + (1,) * (drawn.ndim - 1 - position))

    near = jax.random.permutation(key, shards_of)[block_of(target)]
    other_side = (block_of(target) + shards_of // 2) % shards_of
    return jnp.where((block_of(source) == near) | (block_of(source) == other_side), factor * drawn, drawn)


def block_levels(own_key, dims, cuts, low, top_value):
    def one(axis_at, shards_of):
        draws = jax.random.uniform(jax.random.fold_in(jax.random.fold_in(own_key, 6), axis_at), (shards_of,), jnp.float32, low / len(cuts), top_value / len(cuts))
        return jnp.repeat(jnp.exp(draws), dims[axis_at] // shards_of).reshape((-1,) + (1,) * (len(dims) - axis_at - 1))

    level = one(*cuts[0])
    for cut in cuts[1:]:
        level = level * one(*cut)
    return level


def cumulative_ranks(count, skew):
    weights = [(1 << 20) // math.isqrt(standing ** skew) + 1 for standing in range(1, count + 1)]
    scale = 1 + sum(weights) // (1 << 30)
    return np.cumsum(np.array([max(1, weight // scale) for weight in weights]))


def ranked_ids(rng, shape, amount, skew):
    grid = cumulative_ranks(amount, skew)
    pick = jax.random.randint(jax.random.fold_in(rng, 1), shape, 0, int(grid[amount - 1]))
    grade = jnp.searchsorted(jnp.asarray(grid, jnp.int32), pick, side="right")
    return jax.random.permutation(jax.random.fold_in(rng, 2), amount)[grade].astype(jnp.int32)


def scatter_about(own_key, dims, scale, bound, cuts=(), kind=jnp.bfloat16):
    result = jax.random.normal(own_key, dims, jnp.float32) * scale
    if len(cuts) > 0:
        result = block_levels(own_key, dims, cuts, -0.22, 0.18) * result
    return jnp.clip(result, min=-bound, max=bound).astype(kind)


def bell_draw_with(rng, dims, scale, reach, split, heavy, held_as=jnp.bfloat16):
    entries = scale * jax.random.normal(rng, dims, jnp.float32)
    if split:
        entries = entries * block_levels(rng, dims, split, -0.22, 0.18)
    return jnp.clip(strengthened(entries, jax.random.fold_in(rng, 3), *heavy), -reach, reach).astype(held_as)


def setup_inputs(seed: int = 0) -> dict:
    keys = jax.random.split(jax.random.key(seed), 23)
    return {
        "patches": bell_draw_with(keys[0], (IMAGES, L, D), 1.0, 8.0, ((0, 16),), (0, 2, 16, 2.0)),
        "time_bins": with_ends(ranked_ids(keys[1], (IMAGES,), BINS, 1), jax.random.fold_in(keys[1], 3), 0, BINS - 1).astype(jnp.int32),
        "class_ids": with_ends(jax.random.randint(keys[2], (IMAGES,), 0, CLASSES), jax.random.fold_in(keys[2], 1), 0, CLASSES - 1).astype(jnp.int32),
        "encoder_feats": scatter_about(keys[3], (IMAGES, L, E), 1.0, 6.0, ((0, 16),)),
        "cotangent": bell_draw_with(keys[4], (IMAGES, L, D), 0.25, 2.0, ((0, 16),), (0, 2, 16, 2.0)),
        "w_qkv": scatter_about(keys[5], (3, D, D), D ** -0.5, 0.1875, ((1, 16), (2, 2))),
        "w_out": scatter_about(keys[6], (D, D), (D // 16) ** -0.5, 0.75, ((0, 2), (1, 16))),
        "w_up": scatter_about(keys[7], (D, FF), D ** -0.5, 0.1875, ((0, 16), (1, 2))),
        "w_down": scatter_about(keys[8], (FF, D), FF ** -0.5, 0.09375, ((0, 2), (1, 16))),
        "w_ada": scatter_about(keys[9], (6, D, D), D ** -0.5, 0.1875, ((1, 16),)),
        "time_table": scatter_about(keys[10], (BINS, D), 0.7, 4.0, ((1, 16),)),
        "class_table": scatter_about(keys[11], (CLASSES, D), 0.7, 4.0, ((1, 16),)),
        "inner_bias": scatter_about(keys[12], (N_MP, (2 * D + FF) // N_MP), 0.3, 1.75, ((0, 2), (1, 16)), jnp.float32),
        "b_out": scatter_about(keys[13], (D,), 0.3, 1.75, ((0, 16),), jnp.float32),
        "b_down": scatter_about(keys[14], (D,), 0.3, 1.75, ((0, 16),), jnp.float32),
        "b_ada": scatter_about(keys[15], (6, D), 0.3, 1.75, ((1, 16),), jnp.float32),
        "w_first": scatter_about(keys[16], (D, P_SIZE), D ** -0.5, 0.1875, ((1, 32),)),
        "w_second": scatter_about(keys[17], (P_SIZE, P_SIZE), P_SIZE ** -0.5, 0.125, ((1, 32),)),
        "w_third": scatter_about(keys[18], (P_SIZE, E), P_SIZE ** -0.5, 0.125, ((1, 32),)),
        "b_first": scatter_about(keys[19], (P_SIZE,), 0.3, 1.75, ((0, 32),), jnp.float32),
        "b_second": scatter_about(keys[20], (P_SIZE,), 0.3, 1.75, ((0, 32),), jnp.float32),
        "b_third": scatter_about(keys[21], (E,), 0.5, 3.0, ((0, 32),), jnp.float32),
    }


@jax.custom_vjp
def low(v):
    return lax.optimization_barrier(v.astype(jnp.bfloat16)).astype(jnp.float32)

@jax.custom_vjp
def low_back(v):
    return v

def low_keep(v):
    return (low(v), None)

def low_pass(kept, grad):
    return (grad,)

def back_keep(v):
    return (v, None)

def back_low(kept, grad):
    return (low(grad),)
low.defvjp(low_keep, low_pass)
low_back.defvjp(back_keep, back_low)
epsilon = 1e-06
gelu_slope = 0.7978845608028654
gelu_cubic = 0.044715
highest = lax.Precision.HIGHEST

def gelu_tanh(values):
    inside = gelu_slope * (values + gelu_cubic * values * values * values)
    return 0.5 * values * (1.0 + jnp.tanh(inside))

def layer_norm(values):
    center = values - lax.optimization_barrier(jnp.mean(values, axis=-1, keepdims=True))
    return center * lax.rsqrt(lax.optimization_barrier(jnp.mean(center * center, axis=-1, keepdims=True)) + epsilon)

def block_loss(params, inputs, bin_ids, label_ids, features):
    w_qkv, w_out, w_up, w_down, w_ada, time_table, class_table, inner_bias, b_out, b_down, b_ada, w_first, w_second, w_third, b_first, b_second, b_third = params
    image_count, seq_len, width = inputs.shape
    part_width = width // N_MP
    head_count = width // HD
    bias_query = inner_bias[:, :part_width].reshape(width)
    bias_value = inner_bias[:, part_width:2 * part_width].reshape(width)
    bias_units = inner_bias[:, 2 * part_width:].reshape(-1)
    condition = time_table[bin_ids] + class_table[label_ids]
    cond_act = low(jax.nn.silu(condition))
    modulation = low_back(jnp.einsum('bd,tde->bte', cond_act, w_ada, precision=highest) + b_ada)
    shift_one = modulation[:, 0:1, :]
    scale_one = modulation[:, 1:2, :]
    gate_one = modulation[:, 2:3, :]
    shift_two = modulation[:, 3:4, :]
    scale_two = modulation[:, 4:5, :]
    gate_two = modulation[:, 5:6, :]
    act_one = low(layer_norm(inputs) * (1.0 + scale_one) + shift_one)
    qkv_proj = jnp.einsum('bld,tdc->bltc', act_one, w_qkv, precision=highest)
    head_shape = (image_count, seq_len, head_count, HD)
    queries = low(low_back(qkv_proj[:, :, 0] + bias_query)).reshape(head_shape)
    key_heads = low(low_back(qkv_proj[:, :, 1])).reshape(head_shape)
    val_heads = low(low_back(qkv_proj[:, :, 2] + bias_value)).reshape(head_shape)
    scores = low_back(jnp.einsum('bqhd,bkhd->bhqk', queries, key_heads, precision=highest) * float(HD) ** (-0.5))
    attn_probs = jax.nn.softmax(scores, axis=-1)
    mixed_heads = jnp.einsum('bhqk,bkhd->bqhd', low(attn_probs), val_heads, precision=highest)
    mixed_heads = low(low_back(mixed_heads.reshape(image_count, seq_len, width)))
    attention = low_back(jnp.einsum('blc,cd->bld', mixed_heads, w_out, precision=highest) + b_out)
    first_sum = inputs + gate_one * attention
    act_two = low(layer_norm(first_sum) * (1.0 + scale_two) + shift_two)
    hidden = low_back(jnp.einsum('bld,df->blf', act_two, w_up, precision=highest) + bias_units)
    active = low(gelu_tanh(hidden))
    branch = low_back(jnp.einsum('blf,fd->bld', active, w_down, precision=highest) + b_down)
    output = first_sum + gate_two * branch
    proj_input = low_back(low(output)).reshape(image_count * seq_len, width)
    pre_one = low_back(jnp.dot(proj_input, w_first, precision=highest, preferred_element_type=jnp.float32) + b_first)
    act_pone = low(jax.nn.silu(pre_one))
    pre_two = low_back(jnp.dot(act_pone, w_second, precision=highest, preferred_element_type=jnp.float32) + b_second)
    act_ptwo = low(jax.nn.silu(pre_two))
    mapped = low_back(jnp.dot(act_ptwo, w_third, precision=highest, preferred_element_type=jnp.float32) + b_third)
    target = features.reshape(image_count * seq_len, -1)
    inv_map = lax.rsqrt(lax.optimization_barrier(jnp.sum(mapped * mapped, axis=-1)) + epsilon)
    inv_target = lax.rsqrt(lax.optimization_barrier(jnp.sum(target * target, axis=-1)) + epsilon)
    cosine = lax.optimization_barrier(jnp.sum(mapped * target, axis=-1)) * inv_map * inv_target
    return (output, -0.5 * float(D) * jnp.sum(cosine))

def reference(patches, time_bins, class_ids, encoder_feats, cotangent, w_qkv, w_out, w_up, w_down, w_ada, time_table, class_table, inner_bias, b_out, b_down, b_ada, w_first, w_second, w_third, b_first, b_second, b_third):
    params = tuple((weight.astype(jnp.float32) for weight in (w_qkv, w_out, w_up, w_down, w_ada, time_table, class_table, inner_bias, b_out, b_down, b_ada, w_first, w_second, w_third, b_first, b_second, b_third)))
    group_size = min(16, patches.shape[0])
    group_count = patches.shape[0] // group_size

    def regroup(values):
        return values.reshape((group_count, group_size) + values.shape[1:])

    def step(running, group_data):
        group_in, group_bins, group_labels, group_feats, group_cot = group_data

        def local_loss(weights, inputs):
            return block_loss(weights, inputs, group_bins, group_labels, group_feats.astype(jnp.float32))
        (output, loss_value), pullback = jax.vjp(local_loss, params, group_in.astype(jnp.float32))
        grads, grad_in = pullback((group_cot.astype(output.dtype), jnp.ones_like(loss_value)))
        running = jax.tree.map(jnp.add, running, grads)
        return (running, (output.astype(jnp.bfloat16), grad_in))
    zero_grads = jax.tree.map(jnp.zeros_like, params)
    totals, (outputs, grad_inputs) = lax.scan(step, zero_grads, (regroup(patches), regroup(time_bins), regroup(class_ids), regroup(encoder_feats), regroup(cotangent)))
    block_out = outputs.reshape(patches.shape)
    grad_patches = grad_inputs.reshape(patches.shape)
    return (block_out, grad_patches, totals[0], totals[1], totals[2], totals[3], totals[4], totals[5], totals[6], totals[7], totals[8], totals[9], totals[10], totals[11], totals[12], totals[13], totals[14], totals[15], totals[16])
```

```python
import jax
import jax.numpy as jnp
from jax import lax
from jax.experimental import pallas as pl
from jax.experimental.pallas import tpu as pltpu
from jax.sharding import PartitionSpec as P

HD = 72
ROWS = 2
CORES = 2


epsilon = 1e-06
gelu_slope = 0.7978845608028654
gelu_cubic = 0.044715


def layer_norm(values):
    center = values - jnp.mean(values, axis=-1, keepdims=True)
    inverse = lax.rsqrt(jnp.mean(center * center, axis=-1, keepdims=True) + epsilon)
    return (center * inverse, inverse)


def norm_back(incoming, normed, inverse):
    return inverse * (
        incoming
        - jnp.mean(incoming, axis=-1, keepdims=True)
        - normed * jnp.mean(incoming * normed, axis=-1, keepdims=True)
    )


def gelu_tanh(values):
    inside = gelu_slope * (values + gelu_cubic * values * values * values)
    return 0.5 * values * (1.0 + jnp.tanh(inside))


def gelu_grad(values):
    tangent = jnp.tanh(gelu_slope * (values + gelu_cubic * values * values * values))
    return 0.5 * (1.0 + tangent) + 0.5 * values * (1.0 - tangent * tangent) * gelu_slope * (
        1.0 + 3.0 * gelu_cubic * values * values
    )


def silu_grad(values):
    sigma = jax.nn.sigmoid(values)
    return sigma * (1.0 + values * (1.0 - sigma))


def place_pieces(pieces, place, planes, with_side, cuts):
    count = len(pieces)
    _, held, part_rows, columns = pieces[0].shape

    def body(place_ref, *refs):
        turn = pl.program_id(0)
        sources, targets = refs[:count], refs[count:]
        for k in range(count):

            @pl.when(turn == k)
            def _(k=k):
                for target, (start, end) in zip(targets, cuts):
                    target[...] = sources[k][0, start:end].reshape(target.shape)

    def source_map(k):
        def index_map(turn, s, place_ref):
            return jnp.where(turn == k, s, jnp.where(turn < k, 0, planes - 1)), 0, 0, 0

        return index_map

    def target_map(turn, s, place_ref):
        at_row = place_ref[planes] ^ (turn & 1)
        if with_side:
            at_side = place_ref[planes + 2] ^ ((turn >> 1) & 1)
            at_core = place_ref[planes + 1] ^ (turn >> 2)
            return 0, place_ref[s], at_row, at_core, at_side, 0, 0
        return 0, place_ref[s], at_row, place_ref[planes + 1] ^ (turn >> 1), 0, 0

    middle = (2,) if with_side else ()
    blank = (1,) if with_side else ()
    kind = pieces[0].dtype
    return pl.pallas_call(
        body,
        grid_spec=pltpu.PrefetchScalarGridSpec(
            num_scalar_prefetch=1,
            grid=(count, planes),
            in_specs=[
                pl.BlockSpec((1, held, part_rows, columns), source_map(k)) for k in range(count)
            ],
            out_specs=tuple(
                pl.BlockSpec((end - start, 1, 1, 1) + blank + (part_rows, columns), target_map)
                for start, end in cuts
            ),
        ),
        out_shape=tuple(
            jax.ShapeDtypeStruct(
                (end - start, planes, ROWS, CORES) + middle + (part_rows, columns), kind
            )
            for start, end in cuts
        ),
        cost_estimate=pl.CostEstimate(
            flops=0,
            bytes_accessed=4 * count * planes * held * part_rows * columns,
            transcendentals=0,
        ),
    )(place, *pieces)


def solution(mesh):
    dp, mp = mesh.shape["dp"], mesh.shape["mp"]
    planes = dp // (ROWS * CORES)

    def swap_x(value):
        return lax.ppermute(value, "mp", [(k, k ^ 1) for k in range(mp)])

    def swap_c(value):
        return lax.ppermute(value, "dp", [(k, k ^ 1) for k in range(dp)])

    def swap_y(value):
        return lax.ppermute(value, "dp", [(k, k ^ CORES) for k in range(dp)])

    def shift_z(value, step):
        inner = ROWS * CORES
        pairs = [(k, (k // inner + step) % planes * inner + k % inner) for k in range(dp)]
        return lax.ppermute(value, "dp", pairs)

    def shards(
        patches,
        time_bins,
        class_ids,
        encoder_feats,
        cotangent,
        w_qkv,
        w_out,
        w_up,
        w_down,
        w_ada,
        time_table,
        class_table,
        inner_bias,
        b_out,
        b_down,
        b_ada,
        w_first,
        w_second,
        w_third,
        b_first,
        b_second,
        b_third,
    ):
        f32 = jnp.float32
        bf16 = jnp.bfloat16
        image_count, seq_len, width = patches.shape
        me = lax.axis_index("dp")
        side = lax.axis_index("mp")
        core = lax.rem(me, CORES)
        row = lax.rem(me // CORES, ROWS)
        plane = me // (ROWS * CORES)
        place = jnp.stack(
            [lax.rem(plane - s + planes, planes) for s in range(planes)] + [row, core, side]
        ).astype(jnp.int32)

        def pick(values, index, axis=0):
            return lax.dynamic_index_in_dim(values, index, axis, keepdims=False)

        def both(own):
            other = swap_x(own)
            first = side == 0
            return jnp.stack((jnp.where(first, own, other), jnp.where(first, other, own)), axis=0)

        def gather(shard, following, with_side, cuts):
            held, part_rows, columns = shard.shape
            near = jnp.stack([shard] + [shift_z(shard, s) for s in range(1, planes)], axis=0)
            if following is not None:
                near, following = lax.optimization_barrier((near, following))
            pieces = [near, swap_y(near)]
            if with_side:
                pieces = pieces + [swap_x(piece) for piece in pieces]
            pieces = pieces + [swap_c(piece) for piece in pieces]
            placed = place_pieces(pieces, place, planes, with_side, cuts)
            total = dp * (mp if with_side else 1)
            full = [
                out.reshape(end - start, total * part_rows, columns)
                for out, (start, end) in zip(placed, cuts)
            ]
            return full, following

        def scatter(sums, with_side):
            columns = sums.shape[-1]
            middle = (mp,) if with_side else ()
            cut = sums.reshape((planes, ROWS, CORES) + middle + (-1, columns))
            from_core = swap_c(pick(cut, 1 - core, 2))
            mine = pick(cut, core, 2)
            terms = [mine, from_core]
            if with_side:
                outgoing = sum(pick(term, 1 - side, 2).astype(f32) for term in terms).astype(bf16)
                terms = [pick(term, side, 2) for term in terms] + [swap_x(outgoing)]
            outgoing = sum(pick(term, 1 - row, 1).astype(f32) for term in terms).astype(bf16)
            terms = [pick(term, row, 1) for term in terms] + [swap_y(outgoing)]

            def total(index):
                return sum(pick(term, index, 0).astype(f32) for term in terms)

            result = total(plane)
            for s in range(1, planes):
                outgoing = total(lax.rem(plane + s, planes)).astype(bf16)
                result = result + shift_z(outgoing, s).astype(f32)
            return result

        def gather_near(value, axis):
            value = jnp.concatenate(
                [value] + [shift_z(value, s) for s in range(1, planes)], axis=axis
            )
            value = jnp.concatenate((value, swap_y(value)), axis=axis)
            return jnp.concatenate((value, swap_c(value)), axis=axis)

        lanes = 128
        numbers = jnp.concatenate((time_bins, class_ids)).astype(f32)
        packed = jnp.concatenate(
            (
                jnp.pad(numbers, (0, lanes - numbers.shape[0])),
                inner_bias.reshape(-1),
                b_out,
                b_down,
                b_first,
                b_second,
                b_third,
            )
        ).reshape(1, -1)
        near_packed = gather_near(packed, 0)
        near_ids = near_packed[:, : 2 * image_count].astype(jnp.int32)
        near_bins = near_ids[:, :image_count].reshape(-1)
        near_labels = near_ids[:, image_count:].reshape(-1)
        order = jnp.arange(dp)
        distance = (
            (core ^ (order % CORES)) * ROWS + (row ^ (order // CORES % ROWS))
        ) * planes + (plane - order // (CORES * ROWS)) % planes
        spread = (distance[:, None] == order[None, :]).astype(bf16)
        biases = jnp.dot(
            spread, near_packed[:, lanes:].astype(bf16), preferred_element_type=f32
        )
        inner_size = inner_bias.shape[1]
        thin = b_out.shape[0]
        flat_inner = biases[:, :inner_size].reshape(-1)
        full_bout = biases[:, inner_size : inner_size + thin].reshape(-1)
        full_bdown = biases[:, inner_size + thin : inner_size + 2 * thin].reshape(-1)
        proj_biases = biases[:, inner_size + 2 * thin :].astype(bf16)
        proj_biases = jnp.moveaxis(both(proj_biases), 0, 1).astype(f32)
        hidden_size = b_first.shape[0]
        bias_one = proj_biases[:, :, :hidden_size].reshape(-1)
        bias_two = proj_biases[:, :, hidden_size : 2 * hidden_size].reshape(-1)
        bias_three = proj_biases[:, :, 2 * hidden_size :].reshape(-1)

        bin_onehot = near_bins[:, None] == jnp.arange(time_table.shape[0], dtype=jnp.int32)[None, :]
        class_onehot = (
            near_labels[:, None] == jnp.arange(class_table.shape[0], dtype=jnp.int32)[None, :]
        )
        condition = jnp.dot(
            bin_onehot.astype(bf16), time_table, preferred_element_type=f32
        ) + jnp.dot(class_onehot.astype(bf16), class_table, preferred_element_type=f32)
        cond_act = jax.nn.silu(condition).astype(bf16)
        local_rows = w_ada.shape[1]
        wide_bias = lax.dynamic_update_slice(
            jnp.zeros((b_ada.shape[0], width), f32), b_ada, (0, me * local_rows)
        )
        partial_mods = (
            jnp.einsum("bd,tde->tbe", cond_act, w_ada, preferred_element_type=f32)
            + wide_bias[:, None, :]
        ).astype(bf16)
        half = partial_mods.shape[1] // 2
        mods = partial_mods[:, :half].astype(f32) + swap_c(partial_mods[:, half:]).astype(f32)
        half = half // 2
        mods = mods[:, :half] + swap_y(mods[:, half:].astype(bf16)).astype(f32)
        modulation = mods[:, :image_count]
        for s in range(1, planes):
            start = (planes - s) * image_count
            outgoing = mods[:, start : start + image_count].astype(bf16)
            modulation = modulation + shift_z(outgoing, s).astype(f32)
        shift_one, scale_one, gate_one, shift_two, scale_two, gate_two = (
            modulation[t][:, None, :] for t in range(6)
        )
        scale_own = pick(scale_one, side)
        gate_one = pick(gate_one, side)
        shift_two = pick(shift_two, side)
        scale_two = pick(scale_two, side)
        gate_two = pick(gate_two, side)

        shard_attn = jnp.concatenate((w_qkv, w_out.T[None]), axis=0)
        shard_up = w_up[None]
        shard_down = w_down.T[None]
        shard_one = w_first.T[None]
        shard_two = w_second.T[None]
        shard_three = w_third.T[None]
        (full_qkv, full_out), shard_up = gather(shard_attn, shard_up, False, ((0, 3), (3, 4)))
        (full_up,), shard_down = gather(shard_up, shard_down, False, ((0, 1),))
        (full_down,), shard_one = gather(shard_down, shard_one, False, ((0, 1),))
        (proj_one,), shard_two = gather(shard_one, shard_two, True, ((0, 1),))
        (proj_two,), shard_three = gather(shard_two, shard_three, True, ((0, 1),))
        (proj_three,), _ = gather(shard_three, None, True, ((0, 1),))
        full_out, full_up, full_down = full_out[0], full_up[0], full_down[0]
        proj_one, proj_two, proj_three = proj_one[0], proj_two[0], proj_three[0]

        local_width = full_qkv.shape[2]
        head_count = local_width // HD
        bias_query = flat_inner[:local_width]
        bias_value = flat_inner[local_width : 2 * local_width]
        bias_units = flat_inner[2 * local_width :]
        score_scale = float(HD) ** (-0.5)

        inputs = patches.astype(f32)
        normed_one, inverse_one = layer_norm(inputs)
        act_one = (normed_one * (1.0 + scale_one) + shift_one).astype(bf16)
        qkv_proj = jnp.einsum("bld,tdc->tblc", act_one, full_qkv, preferred_element_type=f32)
        head_shape = (image_count, seq_len, head_count, HD)
        queries = (qkv_proj[0] + bias_query).astype(bf16).reshape(head_shape)
        key_heads = qkv_proj[1].astype(bf16).reshape(head_shape)
        val_heads = (qkv_proj[2] + bias_value).astype(bf16).reshape(head_shape)
        scores = (
            jnp.einsum("bqhd,bkhd->bhqk", queries, key_heads, preferred_element_type=f32)
            * score_scale
        )
        row_max = jnp.max(scores, axis=-1, keepdims=True)
        shifted = jnp.exp(scores - row_max)
        exp_total = jnp.sum(shifted, axis=-1, keepdims=True)
        log_total = row_max + jnp.log(exp_total)
        attn_probs = (shifted / exp_total).astype(bf16)
        mixed_heads = jnp.einsum(
            "bhqk,bkhd->bqhd", attn_probs, val_heads, preferred_element_type=f32
        )
        mixed_heads = mixed_heads.reshape(image_count, seq_len, local_width).astype(bf16)

        def shared(values, weights, contract):
            def part(image):
                return lax.dot_general(
                    pick(values, image),
                    weights,
                    (((1,), (contract,)), ((), ())),
                    preferred_element_type=f32,
                )

            arrived = swap_x(part(1 - side).astype(bf16))
            return part(side) + arrived.astype(f32)

        attention = shared(mixed_heads, full_out, 1) + full_bout
        first_sum = pick(inputs, side) + gate_one * attention
        normed_two, inverse_two = layer_norm(first_sum)
        act_two = both((normed_two * (1.0 + scale_two) + shift_two).astype(bf16))
        hidden = (
            jnp.einsum("bld,df->blf", act_two, full_up, preferred_element_type=f32) + bias_units
        )
        active = gelu_tanh(hidden).astype(bf16)
        branch = shared(active, full_down, 1) + full_bdown
        output = first_sum + gate_two * branch
        block_out = output.astype(bf16)

        target = pick(encoder_feats, side).astype(f32)

        def dot(left, right, left_axis, right_axis):
            return lax.dot_general(
                left, right, (((left_axis,), (right_axis,)), ((), ())), preferred_element_type=f32
            )

        pre_one = dot(block_out, proj_one, 1, 1) + bias_one
        act_pone = jax.nn.silu(pre_one).astype(bf16)
        pre_two = dot(act_pone, proj_two, 1, 1) + bias_two
        act_ptwo = jax.nn.silu(pre_two).astype(bf16)
        mapped = dot(act_ptwo, proj_three, 1, 1) + bias_three
        inv_map = lax.rsqrt(jnp.sum(mapped * mapped, axis=-1, keepdims=True) + epsilon)
        inv_target = lax.rsqrt(jnp.sum(target * target, axis=-1, keepdims=True) + epsilon)
        cosine = jnp.sum(mapped * target, axis=-1, keepdims=True) * inv_map * inv_target
        loss_weight = -0.5 * float(width)
        grad_mapped = (
            loss_weight * (target * inv_map * inv_target - cosine * inv_map * inv_map * mapped)
        ).astype(bf16)
        sum_wthird = scatter(dot(grad_mapped, act_ptwo, 0, 0).astype(bf16), True)
        grad_bthird = jnp.sum(grad_mapped.astype(f32), axis=0)
        grad_pre_two = (dot(grad_mapped, proj_three, 1, 0) * silu_grad(pre_two)).astype(bf16)
        sum_wsecond = scatter(dot(grad_pre_two, act_pone, 0, 0).astype(bf16), True)
        grad_bsecond = jnp.sum(grad_pre_two.astype(f32), axis=0)
        grad_pre_one = (dot(grad_pre_two, proj_two, 1, 0) * silu_grad(pre_one)).astype(bf16)
        sum_wfirst = scatter(dot(grad_pre_one, block_out, 0, 0).astype(bf16), True)
        grad_bfirst = jnp.sum(grad_pre_one.astype(f32), axis=0)
        grad_feed = dot(grad_pre_one, proj_one, 1, 0).astype(bf16)

        grad_output = pick(cotangent, side).astype(f32) + grad_feed.astype(f32)
        grad_branch = (gate_two * grad_output).astype(bf16)
        grad_gate_two = jnp.sum(grad_output * branch, axis=0)
        grad_bdown = jnp.sum(grad_branch.astype(f32), axis=0)
        grad_branch = both(grad_branch)
        tokens = image_count * seq_len
        grad_active = jnp.einsum("bld,df->blf", grad_branch, full_down, preferred_element_type=f32)
        grad_hidden = (grad_active * gelu_grad(hidden)).astype(bf16)
        grad_bunits = jnp.sum(grad_hidden.astype(f32), axis=(0, 1))

        def flat(values):
            return values.reshape(tokens, values.shape[-1])

        sum_down = scatter(dot(flat(grad_branch), flat(active), 0, 0).astype(bf16), False)
        grad_act_two = shared(grad_hidden, full_up, 1)
        sum_up = scatter(dot(flat(act_two), flat(grad_hidden), 0, 0).astype(bf16), False)
        grad_shift_two = jnp.sum(grad_act_two, axis=0)
        grad_scale_two = jnp.sum(grad_act_two * normed_two, axis=0)
        grad_first_sum = grad_output + norm_back(
            grad_act_two * (1.0 + scale_two), normed_two, inverse_two
        )

        grad_attention = (gate_one * grad_first_sum).astype(bf16)
        grad_gate_one = jnp.sum(grad_first_sum * attention, axis=0)
        grad_bout = jnp.sum(grad_attention.astype(f32), axis=0)
        grad_attention = both(grad_attention)
        sum_out = scatter(dot(flat(grad_attention), flat(mixed_heads), 0, 0).astype(bf16), False)
        grad_mixed = jnp.einsum("bld,dc->blc", grad_attention, full_out, preferred_element_type=f32)
        grad_mixed = grad_mixed.astype(bf16).reshape(head_shape)
        scores = (
            jnp.einsum("bqhd,bkhd->bhqk", queries, key_heads, preferred_element_type=f32)
            * score_scale
        )
        probs_again = jnp.exp(scores - log_total)
        grad_values = jnp.einsum(
            "bhqk,bqhd->bkhd", probs_again.astype(bf16), grad_mixed, preferred_element_type=f32
        )
        grad_probs = jnp.einsum(
            "bqhd,bkhd->bhqk", grad_mixed, val_heads, preferred_element_type=f32
        )
        inner_prod = jnp.sum(probs_again * grad_probs, axis=-1, keepdims=True)
        grad_scores = (probs_again * (grad_probs - inner_prod)).astype(bf16)
        grad_queries = (
            jnp.einsum("bhqk,bkhd->bqhd", grad_scores, key_heads, preferred_element_type=f32)
            * score_scale
        )
        grad_keys = (
            jnp.einsum("bhqk,bqhd->bkhd", grad_scores, queries, preferred_element_type=f32)
            * score_scale
        )
        grad_three = [
            grad.reshape(image_count, seq_len, local_width).astype(bf16)
            for grad in (grad_queries, grad_keys, grad_values)
        ]
        grad_bquery = jnp.sum(grad_three[0].astype(f32), axis=(0, 1))
        grad_bvalue = jnp.sum(grad_three[2].astype(f32), axis=(0, 1))
        grad_wide = jnp.concatenate(grad_three, axis=-1)

        def part_one(image):
            picked = pick(grad_wide, image)
            return sum(
                dot(
                    picked[:, t * local_width : (t + 1) * local_width], full_qkv[t], 1, 1
                )
                for t in range(3)
            )

        arrived = swap_x(part_one(1 - side).astype(bf16))
        grad_act_one = part_one(side) + arrived.astype(f32)
        sum_qkv = scatter(dot(flat(act_one), flat(grad_wide), 0, 0).astype(bf16), False)
        sum_qkv = jnp.stack(
            [sum_qkv[:, t * local_width : (t + 1) * local_width] for t in range(3)], axis=0
        )
        normed_own, inverse_own = pick(normed_one, side), pick(inverse_one, side)
        grad_shift_one = jnp.sum(grad_act_one, axis=0)
        grad_scale_one = jnp.sum(grad_act_one * normed_own, axis=0)
        grad_own = grad_first_sum + norm_back(
            grad_act_one * (1.0 + scale_own), normed_own, inverse_own
        )
        grad_other = swap_x(grad_own.astype(bf16)).astype(f32)
        grad_patches = jnp.stack(
            (
                jnp.where(side == 0, grad_own, grad_other),
                jnp.where(side == 0, grad_other, grad_own),
            ),
            axis=0,
        )

        grad_mods = jnp.stack(
            (
                grad_shift_one,
                grad_scale_one,
                grad_gate_one,
                grad_shift_two,
                grad_scale_two,
                grad_gate_two,
            ),
            axis=0,
        ).astype(bf16)
        near_mods = gather_near(jnp.moveaxis(both(grad_mods), 0, 1), 1)
        mods_total = jnp.sum(near_mods.astype(f32), axis=1)
        sum_bada = lax.dynamic_slice_in_dim(mods_total, me * local_rows, local_rows, 1)
        sum_wada = jnp.einsum("bd,tbe->tde", cond_act, near_mods, preferred_element_type=f32)
        grad_cond = jnp.einsum("tbe,tde->bd", near_mods, w_ada, preferred_element_type=f32)
        grad_cond = grad_cond * silu_grad(condition)
        sum_time = jnp.einsum(
            "bn,bd->nd", bin_onehot.astype(f32), grad_cond, precision=lax.Precision.HIGHEST
        )
        sum_class = jnp.einsum(
            "bn,bd->nd", class_onehot.astype(f32), grad_cond, precision=lax.Precision.HIGHEST
        )

        own_sums = jnp.concatenate(
            (grad_bout, grad_bdown, grad_bfirst, grad_bsecond, grad_bthird)
        )
        own_sums = own_sums + swap_x(own_sums)
        sizes = [thin * dp, thin * dp, grad_bfirst.size, grad_bsecond.size, grad_bthird.size]
        rows_of = []
        start = 0
        for k, size in enumerate(sizes):
            piece = own_sums[start : start + size]
            start += size
            if k < 2:
                rows_of.append(piece.reshape(dp, -1))
            else:
                rows_of.append(pick(piece.reshape(dp, mp, -1), side, 1))
        grad_inner = jnp.concatenate((grad_bquery, grad_bvalue, grad_bunits))
        sums = jnp.concatenate([grad_inner.reshape(dp, -1)] + rows_of, axis=1)
        sums = sums.reshape(planes, ROWS, CORES, 1, -1)
        sums = pick(sums, core, 2) + swap_c(pick(sums, 1 - core, 2))
        sums = pick(sums, row, 1) + swap_y(pick(sums, 1 - row, 1))
        total = pick(sums, plane, 0)
        for s in range(1, planes):
            total = total + shift_z(pick(sums, lax.rem(plane + s, planes), 0), s)
        pieces = []
        start = 0
        for size in (inner_size, thin, thin, hidden_size, hidden_size, b_third.shape[0]):
            pieces.append(total[:, start : start + size])
            start += size
        return (
            both(block_out),
            grad_patches,
            sum_qkv,
            sum_out.T,
            sum_up,
            sum_down.T,
            sum_wada,
            sum_time,
            sum_class,
            pieces[0],
            pieces[1][0],
            pieces[2][0],
            sum_bada,
            sum_wfirst.T,
            sum_wsecond.T,
            sum_wthird.T,
            pieces[3][0],
            pieces[4][0],
            pieces[5][0],
        )

    placed = (
        P("dp", None, None),
        P("dp"),
        P("dp"),
        P("dp", None, None),
        P("dp", None, None),
        P(None, "dp", "mp"),
        P("mp", "dp"),
        P("dp", "mp"),
        P("mp", "dp"),
        P(None, "dp", None),
        P(None, "dp"),
        P(None, "dp"),
        P("mp", "dp"),
        P("dp"),
        P("dp"),
        P(None, "dp"),
        P(None, ("dp", "mp")),
        P(None, ("dp", "mp")),
        P(None, ("dp", "mp")),
        P(("dp", "mp")),
        P(("dp", "mp")),
        P(("dp", "mp")),
    )
    return jax.shard_map(
        shards,
        mesh=mesh,
        in_specs=placed,
        out_specs=(
            P("dp", None, None),
            P("dp", None, None),
            P(None, "dp", "mp"),
            P("mp", "dp"),
            P("dp", "mp"),
            P("mp", "dp"),
            P(None, "dp", None),
            P(None, "dp"),
            P(None, "dp"),
            P("mp", "dp"),
            P("dp"),
            P("dp"),
            P(None, "dp"),
            P(None, ("dp", "mp")),
            P(None, ("dp", "mp")),
            P(None, ("dp", "mp")),
            P(("dp", "mp")),
            P(("dp", "mp")),
            P(("dp", "mp")),
        ),
        check_vma=False,
    )
```

```python
import jax
import jax.numpy as jnp
from jax import lax
from jax.experimental import pallas as pl
from jax.experimental.pallas import tpu as pltpu
from jax.sharding import PartitionSpec as P

HD = 72
ROWS = 2
CORES = 2


epsilon = 1e-06
gelu_slope = 0.7978845608028654
gelu_cubic = 0.044715


def layer_norm(values):
    center = values - jnp.mean(values, axis=-1, keepdims=True)
    inverse = lax.rsqrt(jnp.mean(center * center, axis=-1, keepdims=True) + epsilon)
    return (center * inverse, inverse)


def norm_back(incoming, normed, inverse):
    return inverse * (
        incoming
        - jnp.mean(incoming, axis=-1, keepdims=True)
        - normed * jnp.mean(incoming * normed, axis=-1, keepdims=True)
    )


def gelu_tanh(values):
    inside = gelu_slope * (values + gelu_cubic * values * values * values)
    return 0.5 * values * (1.0 + jnp.tanh(inside))


def gelu_grad(values):
    tangent = jnp.tanh(gelu_slope * (values + gelu_cubic * values * values * values))
    return 0.5 * (1.0 + tangent) + 0.5 * values * (1.0 - tangent * tangent) * gelu_slope * (
        1.0 + 3.0 * gelu_cubic * values * values
    )


def silu_grad(values):
    sigma = jax.nn.sigmoid(values)
    return sigma * (1.0 + values * (1.0 - sigma))


def place_pieces(pieces, place, planes, with_side, cuts):
    count = len(pieces)
    _, held, part_rows, columns = pieces[0].shape
    kind = pieces[0].dtype

    def body(place_ref, *refs):
        sources, targets = refs[:count], refs[count : count + len(cuts)]
        slots, in_sems, out_sems = refs[count + len(cuts) :]
        arriving = [
            pltpu.make_async_copy(sources[k], slots.at[k], in_sems.at[k]) for k in range(count)
        ]
        for copy in arriving:
            copy.start()
        leaving = []
        for k in range(count):
            arriving[k].wait()
            at_row = place_ref[planes] ^ (k & 1)
            if with_side:
                at_side = place_ref[planes + 2] ^ ((k >> 1) & 1)
                at_core = place_ref[planes + 1] ^ (k >> 2)
            else:
                at_core = place_ref[planes + 1] ^ (k >> 1)
            for s in range(planes):
                for j, (start, end) in enumerate(cuts):
                    for t in range(start, end):
                        target = targets[j].at[t - start, place_ref[s], at_row, at_core]
                        if with_side:
                            target = target.at[at_side]
                        copy = pltpu.make_async_copy(
                            slots.at[k, s, t], target, out_sems.at[k, s, t]
                        )
                        copy.start()
                        leaving.append(copy)
        for copy in leaving:
            copy.wait()

    middle = (2,) if with_side else ()
    moved = count * planes * held * part_rows * columns * kind.itemsize
    return pl.pallas_call(
        body,
        in_specs=[pl.BlockSpec(memory_space=pltpu.SMEM)]
        + [pl.BlockSpec(memory_space=pl.ANY)] * count,
        out_specs=tuple(pl.BlockSpec(memory_space=pl.ANY) for _ in cuts),
        out_shape=tuple(
            jax.ShapeDtypeStruct(
                (end - start, planes, ROWS, CORES) + middle + (part_rows, columns), kind
            )
            for start, end in cuts
        ),
        scratch_shapes=[
            pltpu.VMEM((count, planes, held, part_rows, columns), kind),
            pltpu.SemaphoreType.DMA((count,)),
            pltpu.SemaphoreType.DMA((count, planes, held)),
        ],
        compiler_params=pltpu.CompilerParams(vmem_limit_bytes=moved * 5 // 4 + (4 << 20)),
        cost_estimate=pl.CostEstimate(flops=0, bytes_accessed=2 * moved, transcendentals=0),
    )(place, *pieces)


def split_grads(left, rights, core, pairs):
    count, tokens, columns = rights.shape
    rows = left.shape[1]
    part = rows // (pairs * CORES)
    kind = left.dtype

    def body(core_ref, left_ref, right_ref, mine_ref, other_ref, sums):
        sums[...] = lax.dot_general(
            left_ref[...],
            right_ref[0],
            (((0,), (0,)), ((), ())),
            preferred_element_type=jnp.float32,
        )
        mine = core_ref[0]
        for j in range(pairs):
            start = pl.multiple_of((CORES * j + mine) * part, 8)
            mine_ref[0, j] = sums[pl.ds(start, part), :].astype(kind)
            start = pl.multiple_of((CORES * j + 1 - mine) * part, 8)
            other_ref[0, j] = sums[pl.ds(start, part), :].astype(kind)

    out = jax.ShapeDtypeStruct((count, pairs, part, columns), kind)
    spec = pl.BlockSpec((1, pairs, part, columns), lambda k, core_ref: (k, 0, 0, 0))
    return pl.pallas_call(
        body,
        grid_spec=pltpu.PrefetchScalarGridSpec(
            num_scalar_prefetch=1,
            grid=(count,),
            in_specs=[
                pl.BlockSpec((tokens, rows), lambda k, core_ref: (0, 0)),
                pl.BlockSpec((1, tokens, columns), lambda k, core_ref: (k, 0, 0)),
            ],
            out_specs=(spec, spec),
            scratch_shapes=[pltpu.VMEM((rows, columns), jnp.float32)],
        ),
        out_shape=(out, out),
        compiler_params=pltpu.CompilerParams(vmem_limit_bytes=32 << 20),
        cost_estimate=pl.CostEstimate(
            flops=2 * count * tokens * rows * columns,
            bytes_accessed=2 * count * (tokens + rows) * columns,
            transcendentals=0,
        ),
    )(core, left, rights)


def heads_dot(left, right, left_axis, right_axis):
    return lax.dot_general(
        left, right, (((left_axis,), (right_axis,)), ((), ())), preferred_element_type=jnp.float32
    )


def attend(queries, keys, values, seq_len):
    tokens, width = queries.shape
    heads = width // HD
    scale = float(HD) ** (-0.5)

    def body(q_ref, k_ref, v_ref, out_ref, lse_ref):
        for head in range(heads):
            at = pl.ds(head * HD, HD)
            scores = heads_dot(q_ref[:, at], k_ref[:, at], 1, 1) * scale
            top = jnp.max(scores, axis=-1, keepdims=True)
            shifted = jnp.exp(scores - top)
            total = jnp.sum(shifted, axis=-1, keepdims=True)
            lse_ref[:, pl.ds(head, 1)] = top + jnp.log(total)
            probs = (shifted / total).astype(out_ref.dtype)
            out_ref[:, at] = heads_dot(probs, v_ref[:, at], 1, 0).astype(out_ref.dtype)

    block = pl.BlockSpec((seq_len, width), lambda image: (image, 0))
    return pl.pallas_call(
        body,
        grid=(tokens // seq_len,),
        in_specs=[block] * 3,
        out_specs=(block, pl.BlockSpec((seq_len, heads), lambda image: (image, 0))),
        out_shape=(
            jax.ShapeDtypeStruct((tokens, width), queries.dtype),
            jax.ShapeDtypeStruct((tokens, heads), jnp.float32),
        ),
        compiler_params=pltpu.CompilerParams(vmem_limit_bytes=32 << 20),
        cost_estimate=pl.CostEstimate(
            flops=16 * tokens * seq_len * width,
            bytes_accessed=8 * tokens * width,
            transcendentals=tokens * seq_len * heads,
        ),
    )(queries, keys, values)


def attend_back(queries, keys, values, lse, incoming, seq_len):
    tokens, width = queries.shape
    heads = width // HD
    scale = float(HD) ** (-0.5)

    def body(q_ref, k_ref, v_ref, lse_ref, in_ref, out_ref):
        kind = out_ref.dtype
        for head in range(heads):
            at = pl.ds(head * HD, HD)
            q, k, v, g = q_ref[:, at], k_ref[:, at], v_ref[:, at], in_ref[:, at]
            probs = jnp.exp(heads_dot(q, k, 1, 1) * scale - lse_ref[:, pl.ds(head, 1)])
            out_ref[2, :, at] = heads_dot(probs.astype(kind), g, 0, 0).astype(kind)
            grad = heads_dot(g, v, 1, 1)
            inner = jnp.sum(probs * grad, axis=-1, keepdims=True)
            grad = (probs * (grad - inner)).astype(kind)
            out_ref[0, :, at] = (heads_dot(grad, k, 1, 0) * scale).astype(kind)
            out_ref[1, :, at] = (heads_dot(grad, q, 0, 0) * scale).astype(kind)

    block = pl.BlockSpec((seq_len, width), lambda image: (image, 0))
    return pl.pallas_call(
        body,
        grid=(tokens // seq_len,),
        in_specs=[block] * 3
        + [pl.BlockSpec((seq_len, heads), lambda image: (image, 0)), block],
        out_specs=pl.BlockSpec((3, seq_len, width), lambda image: (0, image, 0)),
        out_shape=jax.ShapeDtypeStruct((3, tokens, width), queries.dtype),
        compiler_params=pltpu.CompilerParams(vmem_limit_bytes=32 << 20),
        cost_estimate=pl.CostEstimate(
            flops=32 * tokens * seq_len * width,
            bytes_accessed=16 * tokens * width,
            transcendentals=tokens * seq_len * heads,
        ),
    )(queries, keys, values, lse, incoming)


def solution(mesh):
    dp, mp = mesh.shape["dp"], mesh.shape["mp"]
    planes = dp // (ROWS * CORES)

    far = [1 << k for k in range(dp.bit_length() - 2, 1, -1)]
    near_order = [CORES] + far + [1]

    def swap_x(value):
        return lax.ppermute(value, "mp", [(k, k ^ 1) for k in range(mp)])

    def swap(value, mask):
        return lax.ppermute(value, "dp", [(k, k ^ mask) for k in range(dp)])

    def swap_c(value):
        return swap(value, 1)

    def swap_y(value):
        return swap(value, CORES)

    def shards(
        patches,
        time_bins,
        class_ids,
        encoder_feats,
        cotangent,
        w_qkv,
        w_out,
        w_up,
        w_down,
        w_ada,
        time_table,
        class_table,
        inner_bias,
        b_out,
        b_down,
        b_ada,
        w_first,
        w_second,
        w_third,
        b_first,
        b_second,
        b_third,
    ):
        f32 = jnp.float32
        bf16 = jnp.bfloat16
        image_count, seq_len, width = patches.shape
        me = lax.axis_index("dp")
        side = lax.axis_index("mp")
        core = lax.rem(me, CORES)
        row = lax.rem(me // CORES, ROWS)
        plane = me // (ROWS * CORES)

        def spot(index):
            return sum(mask for k, mask in enumerate(far) if index >> k & 1)

        place = jnp.stack(
            [plane ^ (spot(s) // (ROWS * CORES)) for s in range(planes)] + [row, core, side]
        ).astype(jnp.int32)

        def pick(values, index, axis=0):
            return lax.dynamic_index_in_dim(values, index, axis, keepdims=False)

        def ordered(own, other):
            first = side == 0
            return jnp.stack((jnp.where(first, own, other), jnp.where(first, other, own)), axis=0)

        last = [me]
        air = []

        def tie(value, *arrived):
            return lax.optimization_barrier((value,) + arrived)[0]

        def after(value, *arrived):
            return tie(value, *last, *arrived)

        def mark(value):
            last[:] = [value]
            return value

        def fly(value):
            air.append(value)
            return value

        def land():
            last.extend(air)
            air.clear()

        def join(value, arrived, axis=0):
            value = lax.optimization_barrier((value, arrived, *last))
            return mark(jnp.concatenate(value[:2], axis=axis))

        def gather_place(pieces, with_side, cuts):
            _, _, part_rows, columns = pieces[0].shape
            placed = place_pieces(pieces, place, planes, with_side, cuts)
            total = dp * (mp if with_side else 1)
            return [
                out.reshape(end - start, total * part_rows, columns)
                for out, (start, end) in zip(placed, cuts)
            ]

        class Scatter:
            def __init__(self, sums, with_side):
                self.axes = [mask for mask in far] + [CORES, 1] + ([0] if with_side else [])
                shape = (2,) * len(self.axes) + (-1, sums[0].shape[-1])
                self.terms = [[part.reshape(shape)] for part in sums]

            @classmethod
            def from_halves(cls, mine, other):
                self = cls.__new__(cls)
                self.axes = [mask for mask in far] + [CORES]
                shape = (2,) * len(self.axes) + mine.shape[2:]
                arrived = fly(swap_c(other))
                self.terms = [
                    [mine[k].reshape(shape), arrived[k].reshape(shape)]
                    for k in range(mine.shape[0])
                ]
                return self

            def send(self, mask, turn=0, turns=1):
                at = self.axes.index(mask)
                mine = lax.rem(me // mask, 2) if mask else side
                move = (lambda value: swap(value, mask)) if mask else swap_x
                planes_left = 1 << sum(1 for axis in self.axes if axis in far and axis != mask)
                if turn == 0:
                    self.flying = []
                self.terms[0][-1] = after(self.terms[0][-1])
                outgoing = []
                for terms in self.terms:
                    halves = [pick(term, 1 - mine, at) for term in terms]
                    shape = halves[0].shape
                    if turns > 1:
                        size = planes_left // turns
                        halves = [
                            half.reshape((planes_left, -1) + shape[-2:])[
                                turn * size : (turn + 1) * size
                            ]
                            for half in halves
                        ]
                    outgoing.append(sum(half.astype(f32) for half in halves).astype(bf16))
                self.flying.append(fly(move(mark(jnp.stack(outgoing, axis=0)))))
                if turn < turns - 1:
                    return
                arrived = self.flying[0]
                if turns > 1:
                    arrived = jnp.concatenate(self.flying, axis=1)
                    arrived = arrived.reshape((-1,) + shape)
                self.axes.pop(at)
                self.terms = [
                    [pick(term, mine, at) for term in terms] + [arrived[k]]
                    for k, terms in enumerate(self.terms)
                ]

            def finish(self):
                return [sum(term.astype(f32) for term in terms) for terms in self.terms]

        def gather_near(value, axis):
            for mask in near_order:
                value = jnp.concatenate((value, swap(value, mask)), axis=axis)
            return value

        hidden_size = b_first.shape[0]
        shard_late = jnp.concatenate((w_second.T, w_third.T), axis=0)

        lanes = 128
        numbers = jnp.concatenate((time_bins, class_ids)).astype(f32)
        packed = jnp.concatenate(
            (
                jnp.pad(numbers, (0, lanes - numbers.shape[0])),
                inner_bias.reshape(-1),
                b_out,
                b_down,
                b_first,
                b_second,
                b_third,
            )
        ).reshape(1, -1)
        near_packed = packed
        pair_a = tie(w_qkv[None, :2], packed)
        ways_a = list(far)
        arrived = swap(pair_a, ways_a[0])
        for mask in near_order[:-1]:
            near_packed = join(near_packed, swap(near_packed, mask))
            if mask in far and len(ways_a) > 1:
                pair_a = join(pair_a, arrived)
                ways_a.pop(0)
                arrived = swap(pair_a, ways_a[0])
        near_packed = join(near_packed, swap(near_packed, near_order[-1]))
        near_ids = near_packed[:, : 2 * image_count].astype(jnp.int32)
        near_bins = near_ids[:, :image_count].reshape(-1)
        near_labels = near_ids[:, image_count:].reshape(-1)
        order = jnp.arange(dp)
        distance = sum(
            ((me ^ order) // mask % 2) << k for k, mask in enumerate(near_order)
        )
        spread = (distance[:, None] == order[None, :]).astype(bf16)
        biases = jnp.dot(
            spread, near_packed[:, lanes:].astype(bf16), preferred_element_type=f32
        )
        inner_size = inner_bias.shape[1]
        thin = b_out.shape[0]
        flat_inner = biases[:, :inner_size].reshape(-1)
        full_bout = biases[:, inner_size : inner_size + thin].reshape(-1)
        full_bdown = biases[:, inner_size + thin : inner_size + 2 * thin].reshape(-1)
        proj_biases = biases[:, inner_size + 2 * thin :].astype(bf16)
        proj_biases = jnp.moveaxis(ordered(proj_biases, swap_x(proj_biases)), 0, 1).astype(f32)
        bias_one = proj_biases[:, :, :hidden_size].reshape(-1)
        bias_two = proj_biases[:, :, hidden_size : 2 * hidden_size].reshape(-1)
        bias_three = proj_biases[:, :, 2 * hidden_size :].reshape(-1)

        bin_onehot = near_bins[:, None] == jnp.arange(time_table.shape[0], dtype=jnp.int32)[None, :]
        class_onehot = (
            near_labels[:, None] == jnp.arange(class_table.shape[0], dtype=jnp.int32)[None, :]
        )
        condition = jnp.dot(
            bin_onehot.astype(bf16), time_table, preferred_element_type=f32
        ) + jnp.dot(class_onehot.astype(bf16), class_table, preferred_element_type=f32)
        cond_act = jax.nn.silu(condition).astype(bf16)
        local_rows = w_ada.shape[1]
        wide_bias = lax.dynamic_update_slice(
            jnp.zeros((b_ada.shape[0], width), f32), b_ada, (0, me * local_rows)
        )
        partial_mods = (
            jnp.einsum("bd,tde->tbe", cond_act, w_ada, preferred_element_type=f32)
            + wide_bias[:, None, :]
        ).astype(bf16)
        mods = partial_mods.astype(f32)
        near_a = join(pair_a, arrived)
        row_a = swap_y(near_a)
        late = lax.all_gather(tie(shard_late, near_a), ("dp", "mp"), axis=0, tiled=False)
        proj_one = lax.all_gather(tie(w_first.T, near_a), ("dp", "mp"), axis=0, tiled=True)

        class Wide:
            def __init__(self, shard):
                self.value = shard
                self.left = list(far)
                self.arrived = swap(shard, self.left[0])

            def step(self):
                while len(self.left) > 1:
                    self.value = join(self.value, self.arrived)
                    self.left.pop(0)
                    self.arrived = swap(self.value, self.left[0])
                return self.value

            def end(self):
                return join(self.step(), self.arrived)

        wide_b = Wide(tie(jnp.concatenate((w_qkv[2:], w_out.T[None]), axis=0)[None], near_a))
        for mask in near_order[::-1]:
            half = mods.shape[1] // 2
            outgoing = mark(after(mods[:, half:]).astype(bf16))
            if mask == far[0]:
                pair_b = wide_b.step()
            mods = mods[:, :half] + after(swap(outgoing, mask)).astype(f32)
        modulation = after(mods)

        near_mods = jnp.stack((pick(modulation, side, 1), pick(modulation, 1 - side, 1)), axis=1)
        shift_one, scale_one = near_mods[0][:, None, :], near_mods[1][:, None, :]
        scale_own = scale_one[0]
        gate_one, shift_two, scale_two, gate_two = (near_mods[t][0:1] for t in range(2, 6))
        inputs = jnp.stack((pick(patches, side), pick(patches, 1 - side)), axis=0).astype(f32)

        near_b = wide_b.end()
        row_b = swap_y(near_b)
        wide_up = Wide(tie(w_up[None, None], pair_b))
        normed_one, inverse_one = layer_norm(inputs)
        act_one = mark((normed_one * (1.0 + scale_one) + shift_one).astype(bf16))

        def four(near, with_row):
            with_row = mark(after(with_row))
            return [near, with_row, swap_c(tie(near, with_row)), swap_c(with_row)]

        def dot(left, right, left_axis, right_axis):
            return lax.dot_general(
                left, right, (((left_axis,), (right_axis,)), ((), ())), preferred_element_type=f32
            )

        pieces_a = four(near_a, row_a)
        pair_up = wide_up.step()
        wide_down = Wide(tie(w_down.T[None, None], pair_up))
        (w_qk,) = gather_place(pieces_a, False, ((0, 2),))
        local_width = w_qk.shape[2]
        bias_query = flat_inner[:local_width]
        bias_value = flat_inner[local_width : 2 * local_width]
        bias_units = flat_inner[2 * local_width :]
        tokens = image_count * seq_len

        def flat(values):
            return values.reshape(tokens, values.shape[-1])

        act_flat = flat(act_one)
        qk_in = after(act_flat, w_qk)
        queries = (dot(qk_in, w_qk[0], 1, 0) + bias_query).astype(bf16)
        key_heads = dot(qk_in, w_qk[1], 1, 0).astype(bf16)
        mark(key_heads)
        pieces_b = four(near_b, row_b)
        near_up = wide_up.end()
        row_up = swap_y(near_up)
        w_value, full_out = gather_place(
            four(near_b, row_b), False, ((0, 1), (1, 2))
        )
        w_value, full_out = w_value[0], full_out[0]
        v_in = after(act_flat, w_value)
        val_heads = mark((dot(v_in, w_value, 1, 0) + bias_value).astype(bf16))
        wide_down.step()
        mixed_heads, log_total = attend(after(queries), key_heads, val_heads, seq_len)
        mixed_heads = mark(mixed_heads).reshape(image_count, seq_len, local_width)

        arrived = swap_x(mark(dot(after(mixed_heads[1]), full_out, 1, 1).astype(bf16)))
        attention = dot(after(mixed_heads[0]), full_out, 1, 1) + full_bout
        attention = mark(attention)
        near_down = wide_down.end()
        row_down = swap_y(near_down)
        pieces_up = four(near_up, row_up)
        attention = attention + after(arrived).astype(f32)
        first_sum = inputs[0] + gate_one * attention
        normed_two, inverse_two = layer_norm(first_sum)
        act_two = mark((normed_two * (1.0 + scale_two) + shift_two).astype(bf16))
        other_two = swap_x(act_two)
        (full_up,) = gather_place(pieces_up, False, ((0, 1),))
        full_up = mark(full_up[0])

        def feed(values):
            hidden = dot(after(values), full_up, 1, 0) + bias_units
            return hidden, mark(gelu_tanh(hidden).astype(bf16))

        hidden_own, active_own = feed(act_two)
        late_two = after(late)
        proj_two = mark(late_two[:, :hidden_size].reshape(dp * mp * hidden_size, -1))
        proj_three = mark(late_two[:, hidden_size:].reshape(dp * mp * b_third.shape[0], -1))
        hidden_other, active_other = feed(other_two)
        (full_down,) = gather_place(
            four(near_down, row_down), False, ((0, 1),)
        )
        full_down = mark(full_down[0])
        arrived = swap_x(mark(dot(after(active_other), full_down, 1, 1).astype(bf16)))
        branch = mark(dot(after(active_own), full_down, 1, 1))
        branch = branch + full_bdown + after(arrived).astype(f32)
        output = first_sum + gate_two * branch
        block_out = mark(output.astype(bf16))
        other_out = swap_x(block_out)

        target = pick(encoder_feats, side).astype(f32)
        pre_one = dot(after(block_out), proj_one, 1, 1) + bias_one
        act_pone = mark(jax.nn.silu(pre_one).astype(bf16))
        pre_two = dot(after(act_pone), proj_two, 1, 1) + bias_two
        act_ptwo = mark(jax.nn.silu(pre_two).astype(bf16))
        mapped = dot(after(act_ptwo), proj_three, 1, 1) + bias_three
        inv_map = lax.rsqrt(jnp.sum(mapped * mapped, axis=-1, keepdims=True) + epsilon)
        inv_target = lax.rsqrt(jnp.sum(target * target, axis=-1, keepdims=True) + epsilon)
        cosine = jnp.sum(mapped * target, axis=-1, keepdims=True) * inv_map * inv_target
        loss_weight = -0.5 * float(width)
        grad_mapped = mark(
            (
                loss_weight
                * (target * inv_map * inv_target - cosine * inv_map * inv_map * mapped)
            ).astype(bf16)
        )
        grad_bthird = jnp.sum(grad_mapped.astype(f32), axis=0)
        three = Scatter([mark(dot(after(grad_mapped), act_ptwo, 0, 0).astype(bf16))], True)
        fly(other_out)
        land()
        three.send(1)
        grad_pre_two = mark(
            (dot(after(grad_mapped), proj_three, 1, 0) * silu_grad(pre_two)).astype(bf16)
        )
        grad_bsecond = jnp.sum(grad_pre_two.astype(f32), axis=0)
        two = Scatter([mark(dot(after(grad_pre_two), act_pone, 0, 0).astype(bf16))], True)
        land()
        two.send(1)
        three.send(CORES)
        grad_pre_one = mark(
            (dot(after(grad_pre_two), proj_two, 1, 0) * silu_grad(pre_one)).astype(bf16)
        )
        grad_bfirst = jnp.sum(grad_pre_one.astype(f32), axis=0)
        grad_feed = mark(dot(after(grad_pre_one), proj_one, 1, 0))

        grad_output = pick(cotangent, side).astype(f32) + grad_feed.astype(bf16).astype(f32)
        grad_branch = mark((gate_two * grad_output).astype(bf16))
        grad_gate_two = jnp.sum(grad_output * branch, axis=0)
        grad_bdown = jnp.sum(grad_branch.astype(f32), axis=0)
        land()
        other_branch = fly(swap_x(grad_branch))
        two.send(CORES, 0, 4)
        one = Scatter([mark(dot(after(grad_pre_one), block_out, 0, 0).astype(bf16))], True)

        def feed_back(incoming, hidden):
            grad_active = dot(after(incoming), full_down, 1, 0)
            return mark((grad_active * gelu_grad(hidden)).astype(bf16))

        hidden_grad_own = feed_back(grad_branch, hidden_own)
        land()
        three.send(0)
        two.send(CORES, 1, 4)
        one.send(1)
        hidden_grad_other = feed_back(other_branch, hidden_other)
        outgoing = mark(dot(after(hidden_grad_other), full_up, 1, 1).astype(bf16))
        land()
        arrived = fly(swap_x(outgoing))
        three.send(far[-1])
        two.send(CORES, 2, 4)
        grad_act_two = mark(dot(after(hidden_grad_own), full_up, 1, 1))
        grad_bunits = jnp.sum(hidden_grad_own.astype(f32), axis=0) + jnp.sum(
            hidden_grad_other.astype(f32), axis=0
        )
        branch_both = jnp.concatenate((grad_branch, other_branch), axis=0)
        active_both = jnp.concatenate((active_own, active_other), axis=0)
        grad_wdown = mark(dot(after(branch_both), active_both, 0, 0).astype(bf16))
        own_down = lax.psum_scatter(grad_wdown, "dp", scatter_dimension=0, tiled=True)
        land()
        two.send(CORES, 3, 4)
        for mask in far[-2::-1]:
            three.send(mask)
        grad_act_two = after(grad_act_two) + arrived.astype(f32)
        grad_shift_two = jnp.sum(grad_act_two, axis=0)
        grad_scale_two = jnp.sum(grad_act_two * normed_two, axis=0)
        grad_first_sum = grad_output + norm_back(
            grad_act_two * (1.0 + scale_two), normed_two, inverse_two
        )

        grad_attention = mark((gate_one * grad_first_sum).astype(bf16))
        grad_gate_one = jnp.sum(grad_first_sum * attention, axis=0)
        grad_bout = jnp.sum(grad_attention.astype(f32), axis=0)
        land()
        other_attention = fly(swap_x(grad_attention))
        act_both = jnp.concatenate((act_two, other_two), axis=0)
        hidden_both = jnp.concatenate((hidden_grad_own, hidden_grad_other), axis=0)
        grad_wup = mark(dot(after(act_both), hidden_both, 0, 0).astype(bf16))
        own_up = lax.psum_scatter(grad_wup, "dp", scatter_dimension=0, tiled=True)
        land()
        two.send(0, 0, 2)
        attention_both = mark(
            jnp.concatenate((after(grad_attention), other_attention), axis=0)
        )
        grad_mixed = mark(dot(after(attention_both), full_out, 1, 0).astype(bf16))
        my_core = core[None].astype(jnp.int32)
        halves = split_grads(
            after(attention_both), flat(mixed_heads)[None], my_core, planes * ROWS
        )
        out = Scatter.from_halves(halves[0], mark(halves[1]))
        land()
        two.send(0, 1, 2)
        grad_three = mark(
            attend_back(queries, key_heads, val_heads, log_total, after(grad_mixed), seq_len)
        )
        grad_bquery = jnp.sum(grad_three[0].astype(f32), axis=0)
        grad_bvalue = jnp.sum(grad_three[2].astype(f32), axis=0)
        land()
        out.send(CORES)
        two.send(far[-1])

        def part_one(start):
            held = after(grad_three)
            return sum(
                dot(held[t, start : start + seq_len], weight, 1, 1)
                for t, weight in enumerate((w_qk[0], w_qk[1], w_value))
            )

        outgoing = mark(part_one(seq_len).astype(bf16))
        grad_act_one = mark(part_one(0))
        land()
        arrived = fly(swap_x(outgoing))
        one.send(CORES, 0, 2)
        halves = split_grads(act_flat, after(grad_three), my_core, planes * ROWS)
        qkv = Scatter.from_halves(halves[0], mark(halves[1]))
        land()
        one.send(CORES, 1, 2)
        out.send(far[-1])
        normed_own, inverse_own = normed_one[0], inverse_one[0]
        grad_act_one = after(grad_act_one) + arrived.astype(f32)
        grad_shift_one = jnp.sum(grad_act_one, axis=0)
        grad_scale_one = jnp.sum(grad_act_one * normed_own, axis=0)
        grad_own = grad_first_sum + norm_back(
            grad_act_one * (1.0 + scale_own), normed_own, inverse_own
        )
        def rows_of(values):
            short = -values.size % width
            return jnp.pad(values, (0, short)).reshape(-1, width)

        grad_inner = jnp.concatenate((grad_bquery, grad_bvalue, grad_bunits))
        sent = [
            jnp.stack(
                (
                    grad_shift_one,
                    grad_scale_one,
                    grad_gate_one,
                    grad_shift_two,
                    grad_scale_two,
                    grad_gate_two,
                ),
                axis=0,
            )
        ] + [
            rows_of(values)
            for values in (
                grad_bout,
                grad_bdown,
                grad_bfirst,
                grad_bsecond,
                grad_bthird,
                grad_inner,
            )
        ]
        heights = [piece.shape[0] for piece in sent]
        sent = jnp.concatenate(sent, axis=0).astype(bf16)
        mark(sent)
        land()
        row_sent = fly(swap(sent, near_order[0]))
        land()
        qkv.send(CORES)
        near_sent = mark(jnp.stack((after(sent), row_sent), axis=1))
        side_sent = swap_x(near_sent)
        grad_other = fly(swap_x(tie(grad_own.astype(bf16), near_sent)))
        near_sent = ordered(near_sent, after(side_sent))
        near_sent = mark(jnp.moveaxis(near_sent, 0, 2).reshape(sent.shape[0], -1, width))
        arrived = swap(near_sent, near_order[1])
        for mask in far[-2::-1]:
            two.send(mask)
        near_sent = mark(jnp.concatenate((near_sent, after(arrived)), axis=1))
        land()
        arrived = fly(swap(near_sent, near_order[2]))
        one.send(0)
        qkv.send(far[-1])
        for mask in far[-2::-1]:
            out.send(mask)
        land()
        near_sent = mark(jnp.concatenate((after(near_sent), arrived), axis=1))
        for mask in near_order[3:]:
            arrived = fly(swap(near_sent, mask))
            near_sent = mark(jnp.concatenate((near_sent, after(arrived)), axis=1))
        one.send(far[-1])
        for mask in far[-2::-1]:
            qkv.send(mask)
        land()
        for mask in far[-2::-1]:
            one.send(mask)
        near_sent = after(near_sent)
        every_mods = near_sent[: heights[0]]
        totals = jnp.sum(near_sent.astype(f32), axis=1)
        by_side = near_sent.reshape(near_sent.shape[0], dp, mp, width)[-heights[-1] :]
        inner_total = jnp.sum(pick(by_side, side, 2).astype(f32), axis=1).reshape(-1)
        sum_bada = lax.dynamic_slice_in_dim(
            totals[: heights[0]], me * local_rows, local_rows, 1
        )

        def own_part(index, count, parts):
            start = sum(heights[: index + 1])
            values = totals[start : start + heights[index + 1]].reshape(-1)
            at = me if parts == dp else me * mp + side
            return lax.dynamic_slice_in_dim(values, at * count, count, 0)

        sum_bout = own_part(0, thin, dp)
        sum_bdown = own_part(1, thin, dp)
        sum_bfirst = own_part(2, hidden_size, dp * mp)
        sum_bsecond = own_part(3, hidden_size, dp * mp)
        sum_bthird = own_part(4, b_third.shape[0], dp * mp)
        sum_inner = lax.dynamic_slice_in_dim(inner_total, me * inner_size, inner_size, 0)[None]
        sum_wada = jnp.einsum("bd,tbe->tde", cond_act, every_mods, preferred_element_type=f32)
        grad_cond = jnp.einsum("tbe,tde->bd", every_mods, w_ada, preferred_element_type=f32)
        grad_cond = grad_cond * silu_grad(condition)
        sum_time = jnp.einsum(
            "bn,bd->nd", bin_onehot.astype(f32), grad_cond, precision=lax.Precision.HIGHEST
        )
        sum_class = jnp.einsum(
            "bn,bd->nd", class_onehot.astype(f32), grad_cond, precision=lax.Precision.HIGHEST
        )

        (sum_wfirst,) = one.finish()
        sum_down = after(own_down).astype(f32)
        sum_up = after(own_up).astype(f32)
        (sum_wsecond,) = two.finish()
        (sum_wthird,) = three.finish()
        sum_attn = qkv.finish() + out.finish()
        return (
            ordered(block_out, tie(other_out, sum_wada)),
            ordered(grad_own, grad_other.astype(f32)),
            jnp.stack(sum_attn[:3], axis=0),
            sum_attn[3].T,
            sum_up,
            sum_down.T,
            sum_wada,
            sum_time,
            sum_class,
            sum_inner,
            sum_bout,
            sum_bdown,
            sum_bada,
            sum_wfirst.T,
            sum_wsecond.T,
            sum_wthird.T,
            sum_bfirst,
            sum_bsecond,
            sum_bthird,
        )

    placed = (
        P("dp", None, None),
        P("dp"),
        P("dp"),
        P("dp", None, None),
        P("dp", None, None),
        P(None, "dp", "mp"),
        P("mp", "dp"),
        P("dp", "mp"),
        P("mp", "dp"),
        P(None, "dp", None),
        P(None, "dp"),
        P(None, "dp"),
        P("mp", "dp"),
        P("dp"),
        P("dp"),
        P(None, "dp"),
        P(None, ("dp", "mp")),
        P(None, ("dp", "mp")),
        P(None, ("dp", "mp")),
        P(("dp", "mp")),
        P(("dp", "mp")),
        P(("dp", "mp")),
    )
    return jax.shard_map(
        shards,
        mesh=mesh,
        in_specs=placed,
        out_specs=(
            P("dp", None, None),
            P("dp", None, None),
            P(None, "dp", "mp"),
            P("mp", "dp"),
            P("dp", "mp"),
            P("mp", "dp"),
            P(None, "dp", None),
            P(None, "dp"),
            P(None, "dp"),
            P("mp", "dp"),
            P("dp"),
            P("dp"),
            P(None, "dp"),
            P(None, ("dp", "mp")),
            P(None, ("dp", "mp")),
            P(None, ("dp", "mp")),
            P(("dp", "mp")),
            P(("dp", "mp")),
            P(("dp", "mp")),
        ),
        check_vma=False,
    )
```

```python
import jax
import jax.numpy as jnp
from jax import lax
from jax.experimental import pallas as pl
from jax.experimental.pallas import tpu as pltpu
from jax.sharding import PartitionSpec as P

HD = 72
ROWS = 2
CORES = 2


epsilon = 1e-06
gelu_slope = 0.7978845608028654
gelu_cubic = 0.044715


def layer_norm(values):
    center = values - jnp.mean(values, axis=-1, keepdims=True)
    inverse = lax.rsqrt(jnp.mean(center * center, axis=-1, keepdims=True) + epsilon)
    return (center * inverse, inverse)


def norm_back(incoming, normed, inverse):
    return inverse * (
        incoming
        - jnp.mean(incoming, axis=-1, keepdims=True)
        - normed * jnp.mean(incoming * normed, axis=-1, keepdims=True)
    )


def gelu_tanh(values):
    inside = gelu_slope * (values + gelu_cubic * values * values * values)
    return 0.5 * values * (1.0 + jnp.tanh(inside))


def gelu_grad(values):
    tangent = jnp.tanh(gelu_slope * (values + gelu_cubic * values * values * values))
    return 0.5 * (1.0 + tangent) + 0.5 * values * (1.0 - tangent * tangent) * gelu_slope * (
        1.0 + 3.0 * gelu_cubic * values * values
    )


def silu_grad(values):
    sigma = jax.nn.sigmoid(values)
    return sigma * (1.0 + values * (1.0 - sigma))


def place_pieces(pieces, place, planes, with_side, cuts):
    count = len(pieces)
    _, held, part_rows, columns = pieces[0].shape
    kind = pieces[0].dtype

    def body(place_ref, *refs):
        sources, targets = refs[:count], refs[count : count + len(cuts)]
        slots, in_sems, out_sems = refs[count + len(cuts) :]
        arriving = [
            pltpu.make_async_copy(sources[k], slots.at[k], in_sems.at[k]) for k in range(count)
        ]
        for copy in arriving:
            copy.start()
        leaving = []
        for k in range(count):
            arriving[k].wait()
            at_row = place_ref[planes] ^ (k & 1)
            if with_side:
                at_side = place_ref[planes + 2] ^ ((k >> 1) & 1)
                at_core = place_ref[planes + 1] ^ (k >> 2)
            else:
                at_core = place_ref[planes + 1] ^ (k >> 1)
            for s in range(planes):
                for j, (start, end) in enumerate(cuts):
                    for t in range(start, end):
                        target = targets[j].at[t - start, place_ref[s], at_row, at_core]
                        if with_side:
                            target = target.at[at_side]
                        copy = pltpu.make_async_copy(
                            slots.at[k, s, t], target, out_sems.at[k, s, t]
                        )
                        copy.start()
                        leaving.append(copy)
        for copy in leaving:
            copy.wait()

    middle = (2,) if with_side else ()
    moved = count * planes * held * part_rows * columns * kind.itemsize
    return pl.pallas_call(
        body,
        in_specs=[pl.BlockSpec(memory_space=pltpu.SMEM)]
        + [pl.BlockSpec(memory_space=pl.ANY)] * count,
        out_specs=tuple(pl.BlockSpec(memory_space=pl.ANY) for _ in cuts),
        out_shape=tuple(
            jax.ShapeDtypeStruct(
                (end - start, planes, ROWS, CORES) + middle + (part_rows, columns), kind
            )
            for start, end in cuts
        ),
        scratch_shapes=[
            pltpu.VMEM((count, planes, held, part_rows, columns), kind),
            pltpu.SemaphoreType.DMA((count,)),
            pltpu.SemaphoreType.DMA((count, planes, held)),
        ],
        compiler_params=pltpu.CompilerParams(vmem_limit_bytes=moved * 5 // 4 + (4 << 20)),
        cost_estimate=pl.CostEstimate(flops=0, bytes_accessed=2 * moved, transcendentals=0),
    )(place, *pieces)


def split_grads(left, rights, core, pairs):
    count, tokens, columns = rights.shape
    rows = left.shape[1]
    part = rows // (pairs * CORES)
    kind = left.dtype

    def body(core_ref, left_ref, right_ref, mine_ref, other_ref, sums):
        sums[...] = lax.dot_general(
            left_ref[...],
            right_ref[0],
            (((0,), (0,)), ((), ())),
            preferred_element_type=jnp.float32,
        )
        mine = core_ref[0]
        for j in range(pairs):
            start = pl.multiple_of((CORES * j + mine) * part, 8)
            mine_ref[0, j] = sums[pl.ds(start, part), :].astype(kind)
            start = pl.multiple_of((CORES * j + 1 - mine) * part, 8)
            other_ref[0, j] = sums[pl.ds(start, part), :].astype(kind)

    out = jax.ShapeDtypeStruct((count, pairs, part, columns), kind)
    spec = pl.BlockSpec((1, pairs, part, columns), lambda k, core_ref: (k, 0, 0, 0))
    return pl.pallas_call(
        body,
        grid_spec=pltpu.PrefetchScalarGridSpec(
            num_scalar_prefetch=1,
            grid=(count,),
            in_specs=[
                pl.BlockSpec((tokens, rows), lambda k, core_ref: (0, 0)),
                pl.BlockSpec((1, tokens, columns), lambda k, core_ref: (k, 0, 0)),
            ],
            out_specs=(spec, spec),
            scratch_shapes=[pltpu.VMEM((rows, columns), jnp.float32)],
        ),
        out_shape=(out, out),
        compiler_params=pltpu.CompilerParams(vmem_limit_bytes=32 << 20),
        cost_estimate=pl.CostEstimate(
            flops=2 * count * tokens * rows * columns,
            bytes_accessed=2 * count * (tokens + rows) * columns,
            transcendentals=0,
        ),
    )(core, left, rights)


def heads_dot(left, right, left_axis, right_axis):
    return lax.dot_general(
        left, right, (((left_axis,), (right_axis,)), ((), ())), preferred_element_type=jnp.float32
    )


def attend(queries, keys, values, seq_len):
    tokens, width = queries.shape
    heads = width // HD
    scale = float(HD) ** (-0.5)

    def body(q_ref, k_ref, v_ref, out_ref, lse_ref):
        for head in range(heads):
            at = pl.ds(head * HD, HD)
            scores = heads_dot(q_ref[:, at], k_ref[:, at], 1, 1) * scale
            top = jnp.max(scores, axis=-1, keepdims=True)
            shifted = jnp.exp(scores - top)
            total = jnp.sum(shifted, axis=-1, keepdims=True)
            lse_ref[:, pl.ds(head, 1)] = top + jnp.log(total)
            probs = (shifted / total).astype(out_ref.dtype)
            out_ref[:, at] = heads_dot(probs, v_ref[:, at], 1, 0).astype(out_ref.dtype)

    block = pl.BlockSpec((seq_len, width), lambda image: (image, 0))
    return pl.pallas_call(
        body,
        grid=(tokens // seq_len,),
        in_specs=[block] * 3,
        out_specs=(block, pl.BlockSpec((seq_len, heads), lambda image: (image, 0))),
        out_shape=(
            jax.ShapeDtypeStruct((tokens, width), queries.dtype),
            jax.ShapeDtypeStruct((tokens, heads), jnp.float32),
        ),
        compiler_params=pltpu.CompilerParams(vmem_limit_bytes=32 << 20),
        cost_estimate=pl.CostEstimate(
            flops=16 * tokens * seq_len * width,
            bytes_accessed=8 * tokens * width,
            transcendentals=tokens * seq_len * heads,
        ),
    )(queries, keys, values)


def attend_back(queries, keys, values, lse, incoming, seq_len):
    tokens, width = queries.shape
    heads = width // HD
    scale = float(HD) ** (-0.5)

    def body(q_ref, k_ref, v_ref, lse_ref, in_ref, out_ref):
        kind = out_ref.dtype
        for head in range(heads):
            at = pl.ds(head * HD, HD)
            q, k, v, g = q_ref[:, at], k_ref[:, at], v_ref[:, at], in_ref[:, at]
            probs = jnp.exp(heads_dot(q, k, 1, 1) * scale - lse_ref[:, pl.ds(head, 1)])
            out_ref[2, :, at] = heads_dot(probs.astype(kind), g, 0, 0).astype(kind)
            grad = heads_dot(g, v, 1, 1)
            inner = jnp.sum(probs * grad, axis=-1, keepdims=True)
            grad = (probs * (grad - inner)).astype(kind)
            out_ref[0, :, at] = (heads_dot(grad, k, 1, 0) * scale).astype(kind)
            out_ref[1, :, at] = (heads_dot(grad, q, 0, 0) * scale).astype(kind)

    block = pl.BlockSpec((seq_len, width), lambda image: (image, 0))
    return pl.pallas_call(
        body,
        grid=(tokens // seq_len,),
        in_specs=[block] * 3
        + [pl.BlockSpec((seq_len, heads), lambda image: (image, 0)), block],
        out_specs=pl.BlockSpec((3, seq_len, width), lambda image: (0, image, 0)),
        out_shape=jax.ShapeDtypeStruct((3, tokens, width), queries.dtype),
        compiler_params=pltpu.CompilerParams(vmem_limit_bytes=32 << 20),
        cost_estimate=pl.CostEstimate(
            flops=32 * tokens * seq_len * width,
            bytes_accessed=16 * tokens * width,
            transcendentals=tokens * seq_len * heads,
        ),
    )(queries, keys, values, lse, incoming)


def solution(mesh):
    dp, mp = mesh.shape["dp"], mesh.shape["mp"]
    planes = dp // (ROWS * CORES)

    far = [1 << k for k in range(dp.bit_length() - 2, 1, -1)]
    near_order = [CORES] + far + [1]

    def swap_x(value):
        return lax.ppermute(value, "mp", [(k, k ^ 1) for k in range(mp)])

    def swap(value, mask):
        return lax.ppermute(value, "dp", [(k, k ^ mask) for k in range(dp)])

    def swap_c(value):
        return swap(value, 1)

    def swap_y(value):
        return swap(value, CORES)

    def shards(
        patches,
        time_bins,
        class_ids,
        encoder_feats,
        cotangent,
        w_qkv,
        w_out,
        w_up,
        w_down,
        w_ada,
        time_table,
        class_table,
        inner_bias,
        b_out,
        b_down,
        b_ada,
        w_first,
        w_second,
        w_third,
        b_first,
        b_second,
        b_third,
    ):
        f32 = jnp.float32
        bf16 = jnp.bfloat16
        image_count, seq_len, width = patches.shape
        me = lax.axis_index("dp")
        side = lax.axis_index("mp")
        core = lax.rem(me, CORES)
        row = lax.rem(me // CORES, ROWS)
        plane = me // (ROWS * CORES)

        def spot(index):
            return sum(mask for k, mask in enumerate(far) if index >> k & 1)

        place = jnp.stack(
            [plane ^ (spot(s) // (ROWS * CORES)) for s in range(planes)] + [row, core, side]
        ).astype(jnp.int32)

        def pick(values, index, axis=0):
            return lax.dynamic_index_in_dim(values, index, axis, keepdims=False)

        def ordered(own, other):
            first = side == 0
            return jnp.stack((jnp.where(first, own, other), jnp.where(first, other, own)), axis=0)

        last = [me]
        air = []

        def tie(value, *arrived):
            return lax.optimization_barrier((value,) + arrived)[0]

        def after(value, *arrived):
            return tie(value, *last, *arrived)

        def mark(value):
            last[:] = [value]
            return value

        def fly(value):
            air.append(value)
            return value

        def land():
            last.extend(air)
            air.clear()

        def join(value, arrived, axis=0):
            value = lax.optimization_barrier((value, arrived, *last))
            return mark(jnp.concatenate(value[:2], axis=axis))

        def gather_place(pieces, with_side, cuts):
            _, _, part_rows, columns = pieces[0].shape
            placed = place_pieces(pieces, place, planes, with_side, cuts)
            total = dp * (mp if with_side else 1)
            return [
                out.reshape(end - start, total * part_rows, columns)
                for out, (start, end) in zip(placed, cuts)
            ]

        class Scatter:
            def __init__(self, sums, with_side):
                self.axes = [mask for mask in far] + [CORES, 1] + ([0] if with_side else [])
                shape = (2,) * len(self.axes) + (-1, sums[0].shape[-1])
                self.terms = [[part.reshape(shape)] for part in sums]

            @classmethod
            def from_halves(cls, mine, other):
                self = cls.__new__(cls)
                self.axes = [mask for mask in far] + [CORES]
                shape = (2,) * len(self.axes) + mine.shape[2:]
                arrived = fly(swap_c(other))
                self.terms = [
                    [mine[k].reshape(shape), arrived[k].reshape(shape)]
                    for k in range(mine.shape[0])
                ]
                return self

            def send(self, mask, turn=0, turns=1):
                at = self.axes.index(mask)
                mine = lax.rem(me // mask, 2) if mask else side
                move = (lambda value: swap(value, mask)) if mask else swap_x
                planes_left = 1 << sum(1 for axis in self.axes if axis in far and axis != mask)
                if turn == 0:
                    self.flying = []
                self.terms[0][-1] = after(self.terms[0][-1])
                outgoing = []
                for terms in self.terms:
                    halves = [pick(term, 1 - mine, at) for term in terms]
                    shape = halves[0].shape
                    if turns > 1:
                        size = planes_left // turns
                        halves = [
                            half.reshape((planes_left, -1) + shape[-2:])[
                                turn * size : (turn + 1) * size
                            ]
                            for half in halves
                        ]
                    outgoing.append(sum(half.astype(f32) for half in halves).astype(bf16))
                self.flying.append(fly(move(mark(jnp.stack(outgoing, axis=0)))))
                if turn < turns - 1:
                    return
                arrived = self.flying[0]
                if turns > 1:
                    arrived = jnp.concatenate(self.flying, axis=1)
                    arrived = arrived.reshape((-1,) + shape)
                self.axes.pop(at)
                self.terms = [
                    [pick(term, mine, at) for term in terms] + [arrived[k]]
                    for k, terms in enumerate(self.terms)
                ]

            def finish(self):
                return [sum(term.astype(f32) for term in terms) for terms in self.terms]

        def gather_near(value, axis):
            for mask in near_order:
                value = jnp.concatenate((value, swap(value, mask)), axis=axis)
            return value

        hidden_size = b_first.shape[0]
        shard_late = jnp.concatenate((w_second.T, w_third.T), axis=0)

        lanes = 128
        numbers = jnp.concatenate((time_bins, class_ids)).astype(f32)
        packed = jnp.concatenate(
            (
                jnp.pad(numbers, (0, lanes - numbers.shape[0])),
                inner_bias.reshape(-1),
                b_out,
                b_down,
                b_first,
                b_second,
                b_third,
            )
        ).reshape(1, -1)
        near_packed = packed
        pair_a = tie(w_qkv[None, :2], packed)
        ways_a = list(far)
        arrived = swap(pair_a, ways_a[0])
        for mask in near_order[:-1]:
            near_packed = join(near_packed, swap(near_packed, mask))
            if mask in far and len(ways_a) > 1:
                pair_a = join(pair_a, arrived)
                ways_a.pop(0)
                arrived = swap(pair_a, ways_a[0])
        near_packed = join(near_packed, swap(near_packed, near_order[-1]))
        near_ids = near_packed[:, : 2 * image_count].astype(jnp.int32)
        near_bins = near_ids[:, :image_count].reshape(-1)
        near_labels = near_ids[:, image_count:].reshape(-1)
        order = jnp.arange(dp)
        distance = sum(
            ((me ^ order) // mask % 2) << k for k, mask in enumerate(near_order)
        )
        spread = (distance[:, None] == order[None, :]).astype(bf16)
        biases = jnp.dot(
            spread, near_packed[:, lanes:].astype(bf16), preferred_element_type=f32
        )
        inner_size = inner_bias.shape[1]
        thin = b_out.shape[0]
        flat_inner = biases[:, :inner_size].reshape(-1)
        full_bout = biases[:, inner_size : inner_size + thin].reshape(-1)
        full_bdown = biases[:, inner_size + thin : inner_size + 2 * thin].reshape(-1)
        proj_biases = biases[:, inner_size + 2 * thin :].astype(bf16)
        proj_biases = jnp.moveaxis(ordered(proj_biases, swap_x(proj_biases)), 0, 1).astype(f32)
        bias_one = proj_biases[:, :, :hidden_size].reshape(-1)
        bias_two = proj_biases[:, :, hidden_size : 2 * hidden_size].reshape(-1)
        bias_three = proj_biases[:, :, 2 * hidden_size :].reshape(-1)

        bin_onehot = near_bins[:, None] == jnp.arange(time_table.shape[0], dtype=jnp.int32)[None, :]
        class_onehot = (
            near_labels[:, None] == jnp.arange(class_table.shape[0], dtype=jnp.int32)[None, :]
        )
        condition = jnp.dot(
            bin_onehot.astype(bf16), time_table, preferred_element_type=f32
        ) + jnp.dot(class_onehot.astype(bf16), class_table, preferred_element_type=f32)
        cond_act = jax.nn.silu(condition).astype(bf16)
        def near_rows(values):
            cut = values.reshape((-1, ROWS, image_count) + values.shape[1:])
            return cut.swapaxes(1, 2).reshape(values.shape)

        end_rows = [
            near_rows(values) for values in (cond_act, condition, bin_onehot, class_onehot)
        ]
        local_rows = w_ada.shape[1]
        wide_bias = lax.dynamic_update_slice(
            jnp.zeros((b_ada.shape[0], width), f32), b_ada, (0, me * local_rows)
        )
        partial_mods = (
            jnp.einsum("bd,tde->tbe", cond_act, w_ada, preferred_element_type=f32)
            + wide_bias[:, None, :]
        ).astype(bf16)
        mods = partial_mods.astype(f32)
        near_a = join(pair_a, arrived)
        row_a = swap_y(near_a)
        late = lax.all_gather(tie(shard_late, near_a), ("dp", "mp"), axis=0, tiled=False)
        proj_one = lax.all_gather(tie(w_first.T, near_a), ("dp", "mp"), axis=0, tiled=True)

        class Wide:
            def __init__(self, shard):
                self.value = shard
                self.left = list(far)
                self.arrived = swap(shard, self.left[0])

            def step(self):
                while len(self.left) > 1:
                    self.value = join(self.value, self.arrived)
                    self.left.pop(0)
                    self.arrived = swap(self.value, self.left[0])
                return self.value

            def end(self):
                return join(self.step(), self.arrived)

        wide_b = Wide(tie(jnp.concatenate((w_qkv[2:], w_out.T[None]), axis=0)[None], near_a))
        for mask in near_order[::-1]:
            half = mods.shape[1] // 2
            outgoing = mark(after(mods[:, half:]).astype(bf16))
            if mask == far[0]:
                pair_b = wide_b.step()
            mods = mods[:, :half] + after(swap(outgoing, mask)).astype(f32)
        modulation = after(mods)

        near_mods = jnp.stack((pick(modulation, side, 1), pick(modulation, 1 - side, 1)), axis=1)
        shift_one, scale_one = near_mods[0][:, None, :], near_mods[1][:, None, :]
        scale_own = scale_one[0]
        gate_one, shift_two, scale_two, gate_two = (near_mods[t][0:1] for t in range(2, 6))
        inputs = jnp.stack((pick(patches, side), pick(patches, 1 - side)), axis=0).astype(f32)

        near_b = wide_b.end()
        row_b = swap_y(near_b)
        wide_up = Wide(tie(w_up[None, None], pair_b))
        normed_one, inverse_one = layer_norm(inputs)
        act_one = mark((normed_one * (1.0 + scale_one) + shift_one).astype(bf16))
        last.extend(end_rows)

        def four(near, with_row):
            with_row = mark(after(with_row))
            return [near, with_row, swap_c(tie(near, with_row)), swap_c(with_row)]

        def dot(left, right, left_axis, right_axis):
            return lax.dot_general(
                left, right, (((left_axis,), (right_axis,)), ((), ())), preferred_element_type=f32
            )

        pieces_a = four(near_a, row_a)
        pair_up = wide_up.step()
        wide_down = Wide(tie(w_down.T[None, None], pair_up))
        (w_qk,) = gather_place(pieces_a, False, ((0, 2),))
        local_width = w_qk.shape[2]
        bias_query = flat_inner[:local_width]
        bias_value = flat_inner[local_width : 2 * local_width]
        bias_units = flat_inner[2 * local_width :]
        tokens = image_count * seq_len

        def flat(values):
            return values.reshape(tokens, values.shape[-1])

        act_flat = flat(act_one)
        qk_in = after(act_flat, w_qk)
        queries = (dot(qk_in, w_qk[0], 1, 0) + bias_query).astype(bf16)
        key_heads = dot(qk_in, w_qk[1], 1, 0).astype(bf16)
        mark(key_heads)
        pieces_b = four(near_b, row_b)
        near_up = wide_up.end()
        row_up = swap_y(near_up)
        w_value, full_out = gather_place(
            four(near_b, row_b), False, ((0, 1), (1, 2))
        )
        w_value, full_out = w_value[0], full_out[0]
        v_in = after(act_flat, w_value)
        val_heads = mark((dot(v_in, w_value, 1, 0) + bias_value).astype(bf16))
        wide_down.step()
        mixed_heads, log_total = attend(after(queries), key_heads, val_heads, seq_len)
        mixed_heads = mark(mixed_heads).reshape(image_count, seq_len, local_width)

        arrived = swap_x(mark(dot(after(mixed_heads[1]), full_out, 1, 1).astype(bf16)))
        attention = dot(after(mixed_heads[0]), full_out, 1, 1) + full_bout
        attention = mark(attention)
        near_down = wide_down.end()
        row_down = swap_y(near_down)
        pieces_up = four(near_up, row_up)
        attention = attention + after(arrived).astype(f32)
        first_sum = inputs[0] + gate_one * attention
        normed_two, inverse_two = layer_norm(first_sum)
        act_two = mark((normed_two * (1.0 + scale_two) + shift_two).astype(bf16))
        other_two = swap_x(act_two)
        (full_up,) = gather_place(pieces_up, False, ((0, 1),))
        full_up = mark(full_up[0])

        def feed(values):
            hidden = dot(after(values), full_up, 1, 0) + bias_units
            return hidden, mark(gelu_tanh(hidden).astype(bf16))

        hidden_own, active_own = feed(act_two)
        late_two = after(late)
        proj_two = mark(late_two[:, :hidden_size].reshape(dp * mp * hidden_size, -1))
        proj_three = mark(late_two[:, hidden_size:].reshape(dp * mp * b_third.shape[0], -1))
        hidden_other, active_other = feed(other_two)
        (full_down,) = gather_place(
            four(near_down, row_down), False, ((0, 1),)
        )
        full_down = mark(full_down[0])
        arrived = swap_x(mark(dot(after(active_other), full_down, 1, 1).astype(bf16)))
        branch = mark(dot(after(active_own), full_down, 1, 1))
        branch = branch + full_bdown + after(arrived).astype(f32)
        output = first_sum + gate_two * branch
        block_out = mark(output.astype(bf16))
        other_out = swap_x(block_out)

        target = pick(encoder_feats, side).astype(f32)
        pre_one = dot(after(block_out), proj_one, 1, 1) + bias_one
        act_pone = mark(jax.nn.silu(pre_one).astype(bf16))
        pre_two = dot(after(act_pone), proj_two, 1, 1) + bias_two
        act_ptwo = mark(jax.nn.silu(pre_two).astype(bf16))
        mapped = dot(after(act_ptwo), proj_three, 1, 1) + bias_three
        inv_map = lax.rsqrt(jnp.sum(mapped * mapped, axis=-1, keepdims=True) + epsilon)
        inv_target = lax.rsqrt(jnp.sum(target * target, axis=-1, keepdims=True) + epsilon)
        cosine = jnp.sum(mapped * target, axis=-1, keepdims=True) * inv_map * inv_target
        loss_weight = -0.5 * float(width)
        grad_mapped = mark(
            (
                loss_weight
                * (target * inv_map * inv_target - cosine * inv_map * inv_map * mapped)
            ).astype(bf16)
        )
        grad_bthird = jnp.sum(grad_mapped.astype(f32), axis=0, keepdims=True)
        three = Scatter([mark(dot(after(grad_mapped), act_ptwo, 0, 0).astype(bf16))], True)
        fly(other_out)
        land()
        three.send(1)
        grad_pre_two = mark(
            (dot(after(grad_mapped), proj_three, 1, 0) * silu_grad(pre_two)).astype(bf16)
        )
        grad_bsecond = jnp.sum(grad_pre_two.astype(f32), axis=0, keepdims=True)
        two = Scatter([mark(dot(after(grad_pre_two), act_pone, 0, 0).astype(bf16))], True)
        land()
        two.send(1)
        three.send(CORES)
        grad_pre_one = mark(
            (dot(after(grad_pre_two), proj_two, 1, 0) * silu_grad(pre_one)).astype(bf16)
        )
        grad_bfirst = jnp.sum(grad_pre_one.astype(f32), axis=0, keepdims=True)
        grad_feed = mark(dot(after(grad_pre_one), proj_one, 1, 0))

        grad_output = pick(cotangent, side).astype(f32) + grad_feed.astype(bf16).astype(f32)
        grad_branch = mark((gate_two * grad_output).astype(bf16))
        grad_gate_two = jnp.sum(grad_output * branch, axis=0, keepdims=True)
        grad_bdown = jnp.sum(grad_branch.astype(f32), axis=0, keepdims=True)
        land()
        other_branch = fly(swap_x(grad_branch))
        two.send(CORES, 0, 4)
        one = Scatter([mark(dot(after(grad_pre_one), block_out, 0, 0).astype(bf16))], True)

        def feed_back(incoming, hidden):
            grad_active = dot(after(incoming), full_down, 1, 0)
            return mark((grad_active * gelu_grad(hidden)).astype(bf16))

        hidden_grad_own = feed_back(grad_branch, hidden_own)
        land()
        three.send(0)
        two.send(CORES, 1, 4)
        one.send(1)
        hidden_grad_other = feed_back(other_branch, hidden_other)
        outgoing = mark(dot(after(hidden_grad_other), full_up, 1, 1).astype(bf16))
        land()
        arrived = fly(swap_x(outgoing))
        three.send(far[-1])
        two.send(CORES, 2, 4)
        grad_act_two = mark(dot(after(hidden_grad_own), full_up, 1, 1))
        grad_bunits = jnp.sum(hidden_grad_own.astype(f32), axis=0, keepdims=True) + jnp.sum(
            hidden_grad_other.astype(f32), axis=0, keepdims=True
        )
        branch_both = jnp.concatenate((grad_branch, other_branch), axis=0)
        active_both = jnp.concatenate((active_own, active_other), axis=0)
        grad_wdown = mark(dot(after(branch_both), active_both, 0, 0).astype(bf16))
        own_down = lax.psum_scatter(grad_wdown, "dp", scatter_dimension=0, tiled=True)
        land()
        two.send(CORES, 3, 4)
        for mask in far[-2::-1]:
            three.send(mask)
        grad_act_two = after(grad_act_two) + arrived.astype(f32)
        grad_shift_two = jnp.sum(grad_act_two, axis=0, keepdims=True)
        grad_scale_two = jnp.sum(grad_act_two * normed_two, axis=0, keepdims=True)
        grad_first_sum = grad_output + norm_back(
            grad_act_two * (1.0 + scale_two), normed_two, inverse_two
        )

        grad_attention = mark((gate_one * grad_first_sum).astype(bf16))
        grad_gate_one = jnp.sum(grad_first_sum * attention, axis=0, keepdims=True)
        grad_bout = jnp.sum(grad_attention.astype(f32), axis=0, keepdims=True)
        land()
        other_attention = fly(swap_x(grad_attention))
        one.send(CORES, 0, 2)
        act_both = jnp.concatenate((act_two, other_two), axis=0)
        hidden_both = jnp.concatenate((hidden_grad_own, hidden_grad_other), axis=0)
        grad_wup = mark(dot(after(act_both), hidden_both, 0, 0).astype(bf16))
        own_up = lax.psum_scatter(grad_wup, "dp", scatter_dimension=0, tiled=True)
        land()
        two.send(0, 0, 2)
        one.send(CORES, 1, 2)
        attention_both = mark(
            jnp.concatenate((after(grad_attention), other_attention), axis=0)
        )
        grad_mixed = mark(dot(after(attention_both), full_out, 1, 0).astype(bf16))
        my_core = core[None].astype(jnp.int32)
        halves = split_grads(
            after(attention_both), flat(mixed_heads)[None], my_core, planes * ROWS
        )
        out = Scatter.from_halves(halves[0], mark(halves[1]))
        land()
        two.send(0, 1, 2)
        grad_three = mark(
            attend_back(queries, key_heads, val_heads, log_total, after(grad_mixed), seq_len)
        )
        grad_bquery = jnp.sum(grad_three[0].astype(f32), axis=0, keepdims=True)
        grad_bvalue = jnp.sum(grad_three[2].astype(f32), axis=0, keepdims=True)
        land()
        one.send(0)
        out.send(CORES)
        two.send(far[-1])

        def part_one(start):
            held = after(grad_three)
            return sum(
                dot(held[t, start : start + seq_len], weight, 1, 1)
                for t, weight in enumerate((w_qk[0], w_qk[1], w_value))
            )

        outgoing = mark(part_one(seq_len).astype(bf16))
        grad_act_one = mark(part_one(0))
        land()
        arrived = fly(swap_x(outgoing))
        halves = split_grads(act_flat, after(grad_three), my_core, planes * ROWS)
        qkv = Scatter.from_halves(halves[0], mark(halves[1]))
        for mask in far[-2::-1]:
            two.send(mask)
        land()
        one.send(far[-1])
        out.send(far[-1])
        normed_own, inverse_own = normed_one[0], inverse_one[0]
        grad_act_one = after(grad_act_one) + arrived.astype(f32)
        grad_shift_one = jnp.sum(grad_act_one, axis=0, keepdims=True)
        grad_scale_one = jnp.sum(grad_act_one * normed_own, axis=0, keepdims=True)
        grad_own = grad_first_sum + norm_back(
            grad_act_one * (1.0 + scale_own), normed_own, inverse_own
        )
        sent = [
            grad_shift_one,
            grad_scale_one,
            grad_gate_one,
            grad_shift_two,
            grad_scale_two,
            grad_gate_two,
            grad_bout,
            grad_bdown,
            grad_bfirst,
            grad_bsecond,
            grad_bthird,
            grad_bquery,
            grad_bvalue,
            grad_bunits,
        ]
        starts = [0]
        for piece in sent:
            starts.append(starts[-1] + piece.shape[1])
        sent = jnp.concatenate([piece.astype(bf16) for piece in sent], axis=1)
        mark(sent)
        land()
        row_sent = swap(sent, near_order[0])
        qkv.send(CORES)
        for mask in far[-2::-1]:
            one.send(mask)
            out.send(mask)
        near_sent = mark(jnp.concatenate((sent, after(row_sent)), axis=0))
        side_sent = swap_x(near_sent)
        grad_other = swap_x(tie(grad_own.astype(bf16), near_sent))
        near_sent = mark(ordered(near_sent, after(side_sent)).reshape(-1, sent.shape[1]))
        for k, mask in enumerate(near_order[1:]):
            arrived = swap(near_sent, mask)
            near_sent = mark(jnp.concatenate((near_sent, after(arrived)), axis=0))
            if k == 0:
                land()
                qkv.send(far[-1])
        land()
        for mask in far[-2::-1]:
            qkv.send(mask)
        near_sent = after(near_sent)
        def own_part(index, count, parts, values):
            held = values[:, starts[index] : starts[index] + count * parts]
            at = me if parts == dp else me * mp + side
            return lax.dynamic_slice_in_dim(held, at * count, count, 1)

        totals = jnp.sum(near_sent.astype(f32), axis=0, keepdims=True)
        same_side = jnp.arange(near_sent.shape[0]) // ROWS % image_count == side
        inner_total = jnp.sum(
            jnp.where(same_side[:, None], near_sent[:, starts[11] :].astype(f32), 0.0),
            axis=0,
            keepdims=True,
        )
        sum_bada = jnp.concatenate([own_part(t, thin, dp, totals) for t in range(6)], axis=0)
        sum_bout = own_part(6, thin, dp, totals)[0]
        sum_bdown = own_part(7, thin, dp, totals)[0]
        sum_bfirst = own_part(8, hidden_size, dp * mp, totals)[0]
        sum_bsecond = own_part(9, hidden_size, dp * mp, totals)[0]
        sum_bthird = own_part(10, b_third.shape[0], dp * mp, totals)[0]
        sum_inner = lax.dynamic_slice_in_dim(inner_total, me * inner_size, inner_size, 1)
        cond_act, condition, bin_onehot, class_onehot = end_rows
        every_mods = [near_sent[:, starts[t] : starts[t + 1]] for t in range(6)]
        sum_wada = jnp.stack([dot(cond_act, mods, 0, 0) for mods in every_mods], axis=0)
        grad_cond = sum(dot(mods, w_ada[t], 1, 1) for t, mods in enumerate(every_mods))
        grad_cond = grad_cond * silu_grad(condition)
        mark(sum_wada)
        sum_time = jnp.einsum(
            "bn,bd->nd", bin_onehot.astype(f32), grad_cond, precision=lax.Precision.HIGHEST
        )
        sum_class = jnp.einsum(
            "bn,bd->nd", class_onehot.astype(f32), grad_cond, precision=lax.Precision.HIGHEST
        )

        (sum_wfirst,) = one.finish()
        sum_down = after(own_down).astype(f32)
        sum_up = after(own_up).astype(f32)
        (sum_wsecond,) = two.finish()
        (sum_wthird,) = three.finish()
        sum_attn = qkv.finish() + out.finish()
        return (
            ordered(block_out, tie(other_out, sum_wada)),
            ordered(grad_own, grad_other.astype(f32)),
            jnp.stack(sum_attn[:3], axis=0),
            sum_attn[3].T,
            sum_up,
            sum_down.T,
            sum_wada,
            sum_time,
            sum_class,
            sum_inner,
            sum_bout,
            sum_bdown,
            sum_bada,
            sum_wfirst.T,
            sum_wsecond.T,
            sum_wthird.T,
            sum_bfirst,
            sum_bsecond,
            sum_bthird,
        )

    placed = (
        P("dp", None, None),
        P("dp"),
        P("dp"),
        P("dp", None, None),
        P("dp", None, None),
        P(None, "dp", "mp"),
        P("mp", "dp"),
        P("dp", "mp"),
        P("mp", "dp"),
        P(None, "dp", None),
        P(None, "dp"),
        P(None, "dp"),
        P("mp", "dp"),
        P("dp"),
        P("dp"),
        P(None, "dp"),
        P(None, ("dp", "mp")),
        P(None, ("dp", "mp")),
        P(None, ("dp", "mp")),
        P(("dp", "mp")),
        P(("dp", "mp")),
        P(("dp", "mp")),
    )
    return jax.shard_map(
        shards,
        mesh=mesh,
        in_specs=placed,
        out_specs=(
            P("dp", None, None),
            P("dp", None, None),
            P(None, "dp", "mp"),
            P("mp", "dp"),
            P("dp", "mp"),
            P("mp", "dp"),
            P(None, "dp", None),
            P(None, "dp"),
            P(None, "dp"),
            P("mp", "dp"),
            P("dp"),
            P("dp"),
            P(None, "dp"),
            P(None, ("dp", "mp")),
            P(None, ("dp", "mp")),
            P(None, ("dp", "mp")),
            P(("dp", "mp")),
            P(("dp", "mp")),
            P(("dp", "mp")),
        ),
        check_vma=False,
    )
```

```python
import jax
import jax.numpy as jnp
from jax import lax
from jax.experimental import pallas as pl
from jax.experimental.pallas import tpu as pltpu
from jax.sharding import PartitionSpec as P

HD = 72
ROWS = 2
CORES = 2


epsilon = 1e-06
gelu_slope = 0.7978845608028654
gelu_cubic = 0.044715


def layer_norm(values):
    center = values - jnp.mean(values, axis=-1, keepdims=True)
    inverse = lax.rsqrt(jnp.mean(center * center, axis=-1, keepdims=True) + epsilon)
    return (center * inverse, inverse)


def norm_back(incoming, normed, inverse):
    return inverse * (
        incoming
        - jnp.mean(incoming, axis=-1, keepdims=True)
        - normed * jnp.mean(incoming * normed, axis=-1, keepdims=True)
    )


def gelu_tanh(values):
    inside = gelu_slope * (values + gelu_cubic * values * values * values)
    return 0.5 * values * (1.0 + jnp.tanh(inside))


def gelu_grad(values):
    tangent = jnp.tanh(gelu_slope * (values + gelu_cubic * values * values * values))
    return 0.5 * (1.0 + tangent) + 0.5 * values * (1.0 - tangent * tangent) * gelu_slope * (
        1.0 + 3.0 * gelu_cubic * values * values
    )


def silu_grad(values):
    sigma = jax.nn.sigmoid(values)
    return sigma * (1.0 + values * (1.0 - sigma))


def place_pieces(pieces, place, planes, with_side, cuts):
    count = len(pieces)
    _, held, part_rows, columns = pieces[0].shape
    kind = pieces[0].dtype

    def body(place_ref, *refs):
        sources, targets = refs[:count], refs[count : count + len(cuts)]
        slots, in_sems, out_sems = refs[count + len(cuts) :]
        arriving = [
            pltpu.make_async_copy(sources[k], slots.at[k], in_sems.at[k]) for k in range(count)
        ]
        for copy in arriving:
            copy.start()
        leaving = []
        for k in range(count):
            arriving[k].wait()
            at_row = place_ref[planes] ^ (k & 1)
            if with_side:
                at_side = place_ref[planes + 2] ^ ((k >> 1) & 1)
                at_core = place_ref[planes + 1] ^ (k >> 2)
            else:
                at_core = place_ref[planes + 1] ^ (k >> 1)
            for s in range(planes):
                for j, (start, end) in enumerate(cuts):
                    for t in range(start, end):
                        target = targets[j].at[t - start, place_ref[s], at_row, at_core]
                        if with_side:
                            target = target.at[at_side]
                        copy = pltpu.make_async_copy(
                            slots.at[k, s, t], target, out_sems.at[k, s, t]
                        )
                        copy.start()
                        leaving.append(copy)
        for copy in leaving:
            copy.wait()

    middle = (2,) if with_side else ()
    moved = count * planes * held * part_rows * columns * kind.itemsize
    return pl.pallas_call(
        body,
        in_specs=[pl.BlockSpec(memory_space=pltpu.SMEM)]
        + [pl.BlockSpec(memory_space=pl.ANY)] * count,
        out_specs=tuple(pl.BlockSpec(memory_space=pl.ANY) for _ in cuts),
        out_shape=tuple(
            jax.ShapeDtypeStruct(
                (end - start, planes, ROWS, CORES) + middle + (part_rows, columns), kind
            )
            for start, end in cuts
        ),
        scratch_shapes=[
            pltpu.VMEM((count, planes, held, part_rows, columns), kind),
            pltpu.SemaphoreType.DMA((count,)),
            pltpu.SemaphoreType.DMA((count, planes, held)),
        ],
        compiler_params=pltpu.CompilerParams(vmem_limit_bytes=moved * 5 // 4 + (4 << 20)),
        cost_estimate=pl.CostEstimate(flops=0, bytes_accessed=2 * moved, transcendentals=0),
    )(place, *pieces)


def split_grads(left, rights, core, pairs):
    count, tokens, columns = rights.shape
    rows = left.shape[1]
    part = rows // (pairs * CORES)
    kind = left.dtype

    def body(core_ref, left_ref, right_ref, mine_ref, other_ref, sums):
        sums[...] = lax.dot_general(
            left_ref[...],
            right_ref[0],
            (((0,), (0,)), ((), ())),
            preferred_element_type=jnp.float32,
        )
        mine = core_ref[0]
        for j in range(pairs):
            start = pl.multiple_of((CORES * j + mine) * part, 8)
            mine_ref[0, j] = sums[pl.ds(start, part), :].astype(kind)
            start = pl.multiple_of((CORES * j + 1 - mine) * part, 8)
            other_ref[0, j] = sums[pl.ds(start, part), :].astype(kind)

    out = jax.ShapeDtypeStruct((count, pairs, part, columns), kind)
    spec = pl.BlockSpec((1, pairs, part, columns), lambda k, core_ref: (k, 0, 0, 0))
    return pl.pallas_call(
        body,
        grid_spec=pltpu.PrefetchScalarGridSpec(
            num_scalar_prefetch=1,
            grid=(count,),
            in_specs=[
                pl.BlockSpec((tokens, rows), lambda k, core_ref: (0, 0)),
                pl.BlockSpec((1, tokens, columns), lambda k, core_ref: (k, 0, 0)),
            ],
            out_specs=(spec, spec),
            scratch_shapes=[pltpu.VMEM((rows, columns), jnp.float32)],
        ),
        out_shape=(out, out),
        compiler_params=pltpu.CompilerParams(vmem_limit_bytes=32 << 20),
        cost_estimate=pl.CostEstimate(
            flops=2 * count * tokens * rows * columns,
            bytes_accessed=2 * count * (tokens + rows) * columns,
            transcendentals=0,
        ),
    )(core, left, rights)


def heads_dot(left, right, left_axis, right_axis):
    return lax.dot_general(
        left, right, (((left_axis,), (right_axis,)), ((), ())), preferred_element_type=jnp.float32
    )


def attend(queries, keys, values, seq_len):
    tokens, width = queries.shape
    heads = width // HD
    scale = float(HD) ** (-0.5)

    def body(q_ref, k_ref, v_ref, out_ref, lse_ref):
        for head in range(heads):
            at = pl.ds(head * HD, HD)
            scores = heads_dot(q_ref[:, at], k_ref[:, at], 1, 1) * scale
            top = jnp.max(scores, axis=-1, keepdims=True)
            shifted = jnp.exp(scores - top)
            total = jnp.sum(shifted, axis=-1, keepdims=True)
            lse_ref[:, pl.ds(head, 1)] = top + jnp.log(total)
            probs = (shifted / total).astype(out_ref.dtype)
            out_ref[:, at] = heads_dot(probs, v_ref[:, at], 1, 0).astype(out_ref.dtype)

    block = pl.BlockSpec((seq_len, width), lambda image: (image, 0))
    return pl.pallas_call(
        body,
        grid=(tokens // seq_len,),
        in_specs=[block] * 3,
        out_specs=(block, pl.BlockSpec((seq_len, heads), lambda image: (image, 0))),
        out_shape=(
            jax.ShapeDtypeStruct((tokens, width), queries.dtype),
            jax.ShapeDtypeStruct((tokens, heads), jnp.float32),
        ),
        compiler_params=pltpu.CompilerParams(vmem_limit_bytes=32 << 20),
        cost_estimate=pl.CostEstimate(
            flops=16 * tokens * seq_len * width,
            bytes_accessed=8 * tokens * width,
            transcendentals=tokens * seq_len * heads,
        ),
    )(queries, keys, values)


def attend_back(queries, keys, values, lse, incoming, seq_len):
    tokens, width = queries.shape
    heads = width // HD
    scale = float(HD) ** (-0.5)

    def body(q_ref, k_ref, v_ref, lse_ref, in_ref, out_ref):
        kind = out_ref.dtype
        for head in range(heads):
            at = pl.ds(head * HD, HD)
            q, k, v, g = q_ref[:, at], k_ref[:, at], v_ref[:, at], in_ref[:, at]
            probs = jnp.exp(heads_dot(q, k, 1, 1) * scale - lse_ref[:, pl.ds(head, 1)])
            out_ref[2, :, at] = heads_dot(probs.astype(kind), g, 0, 0).astype(kind)
            grad = heads_dot(g, v, 1, 1)
            inner = jnp.sum(probs * grad, axis=-1, keepdims=True)
            grad = (probs * (grad - inner)).astype(kind)
            out_ref[0, :, at] = (heads_dot(grad, k, 1, 0) * scale).astype(kind)
            out_ref[1, :, at] = (heads_dot(grad, q, 0, 0) * scale).astype(kind)

    block = pl.BlockSpec((seq_len, width), lambda image: (image, 0))
    return pl.pallas_call(
        body,
        grid=(tokens // seq_len,),
        in_specs=[block] * 3
        + [pl.BlockSpec((seq_len, heads), lambda image: (image, 0)), block],
        out_specs=pl.BlockSpec((3, seq_len, width), lambda image: (0, image, 0)),
        out_shape=jax.ShapeDtypeStruct((3, tokens, width), queries.dtype),
        compiler_params=pltpu.CompilerParams(vmem_limit_bytes=32 << 20),
        cost_estimate=pl.CostEstimate(
            flops=32 * tokens * seq_len * width,
            bytes_accessed=16 * tokens * width,
            transcendentals=tokens * seq_len * heads,
        ),
    )(queries, keys, values, lse, incoming)


def solution(mesh):
    dp, mp = mesh.shape["dp"], mesh.shape["mp"]
    planes = dp // (ROWS * CORES)

    far = [1 << k for k in range(dp.bit_length() - 2, 1, -1)]
    near_order = [CORES] + far + [1]

    def swap_x(value):
        return lax.ppermute(value, "mp", [(k, k ^ 1) for k in range(mp)])

    def swap(value, mask):
        return lax.ppermute(value, "dp", [(k, k ^ mask) for k in range(dp)])

    def swap_c(value):
        return swap(value, 1)

    def swap_y(value):
        return swap(value, CORES)

    def shards(
        patches,
        time_bins,
        class_ids,
        encoder_feats,
        cotangent,
        w_qkv,
        w_out,
        w_up,
        w_down,
        w_ada,
        time_table,
        class_table,
        inner_bias,
        b_out,
        b_down,
        b_ada,
        w_first,
        w_second,
        w_third,
        b_first,
        b_second,
        b_third,
    ):
        f32 = jnp.float32
        bf16 = jnp.bfloat16
        image_count, seq_len, width = patches.shape
        me = lax.axis_index("dp")
        side = lax.axis_index("mp")
        core = lax.rem(me, CORES)
        row = lax.rem(me // CORES, ROWS)
        plane = me // (ROWS * CORES)

        def spot(index):
            return sum(mask for k, mask in enumerate(far) if index >> k & 1)

        place = jnp.stack(
            [plane ^ (spot(s) // (ROWS * CORES)) for s in range(planes)] + [row, core, side]
        ).astype(jnp.int32)

        def pick(values, index, axis=0):
            return lax.dynamic_index_in_dim(values, index, axis, keepdims=False)

        def ordered(own, other):
            first = side == 0
            return jnp.stack((jnp.where(first, own, other), jnp.where(first, other, own)), axis=0)

        last = [me]
        air = []

        def tie(value, *arrived):
            return lax.optimization_barrier((value,) + arrived)[0]

        def after(value, *arrived):
            return tie(value, *last, *arrived)

        def mark(value):
            last[:] = [value]
            return value

        def fly(value):
            air.append(value)
            return value

        def hold():
            return air.pop()

        def land():
            last.extend(air)
            air.clear()

        def join(value, arrived, axis=0):
            value = lax.optimization_barrier((value, arrived, *last))
            return mark(jnp.concatenate(value[:2], axis=axis))

        def gather_place(pieces, with_side, cuts):
            _, _, part_rows, columns = pieces[0].shape
            placed = place_pieces(pieces, place, planes, with_side, cuts)
            total = dp * (mp if with_side else 1)
            return [
                out.reshape(end - start, total * part_rows, columns)
                for out, (start, end) in zip(placed, cuts)
            ]

        class Scatter:
            def __init__(self, sums, with_side):
                self.axes = [mask for mask in far] + [CORES, 1] + ([0] if with_side else [])
                shape = (2,) * len(self.axes) + (-1, sums[0].shape[-1])
                self.terms = [[part.reshape(shape)] for part in sums]

            @classmethod
            def from_halves(cls, mine, other):
                self = cls.__new__(cls)
                self.axes = [mask for mask in far] + [CORES]
                shape = (2,) * len(self.axes) + mine.shape[2:]
                arrived = fly(swap_c(other))
                self.terms = [
                    [mine[k].reshape(shape), arrived[k].reshape(shape)]
                    for k in range(mine.shape[0])
                ]
                return self

            def send(self, mask, turn=0, turns=1):
                at = self.axes.index(mask)
                mine = lax.rem(me // mask, 2) if mask else side
                move = (lambda value: swap(value, mask)) if mask else swap_x
                planes_left = 1 << sum(1 for axis in self.axes if axis in far and axis != mask)
                if turn == 0:
                    self.flying = []
                self.terms[0][-1] = after(self.terms[0][-1])
                outgoing = []
                for terms in self.terms:
                    halves = [pick(term, 1 - mine, at) for term in terms]
                    shape = halves[0].shape
                    if turns > 1:
                        size = planes_left // turns
                        halves = [
                            half.reshape((planes_left, -1) + shape[-2:])[
                                turn * size : (turn + 1) * size
                            ]
                            for half in halves
                        ]
                    outgoing.append(sum(half.astype(f32) for half in halves).astype(bf16))
                self.flying.append(fly(move(mark(jnp.stack(outgoing, axis=0)))))
                if turn < turns - 1:
                    return
                arrived = self.flying[0]
                if turns > 1:
                    arrived = jnp.concatenate(self.flying, axis=1)
                    arrived = arrived.reshape((-1,) + shape)
                self.axes.pop(at)
                self.terms = [
                    [pick(term, mine, at) for term in terms] + [arrived[k]]
                    for k, terms in enumerate(self.terms)
                ]

            def finish(self):
                return [sum(term.astype(f32) for term in terms) for terms in self.terms]

        def gather_near(value, axis):
            for mask in near_order:
                value = jnp.concatenate((value, swap(value, mask)), axis=axis)
            return value

        hidden_size = b_first.shape[0]
        shard_late = jnp.concatenate((w_second.T, w_third.T), axis=0)

        lanes = 128
        numbers = jnp.concatenate((time_bins, class_ids)).astype(f32)
        packed = jnp.concatenate(
            (
                jnp.pad(numbers, (0, lanes - numbers.shape[0])),
                inner_bias.reshape(-1),
                b_out,
                b_down,
                b_first,
                b_second,
                b_third,
            )
        ).reshape(1, -1)
        near_packed = packed
        pair_a = tie(w_qkv[None, :2], packed)
        ways_a = list(far)
        arrived = swap(pair_a, ways_a[0])
        for mask in near_order[:-1]:
            near_packed = join(near_packed, swap(near_packed, mask))
            if mask in far and len(ways_a) > 1:
                pair_a = join(pair_a, arrived)
                ways_a.pop(0)
                arrived = swap(pair_a, ways_a[0])
        near_packed = join(near_packed, swap(near_packed, near_order[-1]))
        near_ids = near_packed[:, : 2 * image_count].astype(jnp.int32)
        near_bins = near_ids[:, :image_count].reshape(-1)
        near_labels = near_ids[:, image_count:].reshape(-1)
        order = jnp.arange(dp)
        distance = sum(
            ((me ^ order) // mask % 2) << k for k, mask in enumerate(near_order)
        )
        spread = (distance[:, None] == order[None, :]).astype(bf16)
        biases = jnp.dot(
            spread, near_packed[:, lanes:].astype(bf16), preferred_element_type=f32
        )
        inner_size = inner_bias.shape[1]
        thin = b_out.shape[0]
        flat_inner = biases[:, :inner_size].reshape(-1)
        full_bout = biases[:, inner_size : inner_size + thin].reshape(-1)
        full_bdown = biases[:, inner_size + thin : inner_size + 2 * thin].reshape(-1)
        proj_biases = biases[:, inner_size + 2 * thin :].astype(bf16)
        proj_biases = jnp.moveaxis(ordered(proj_biases, swap_x(proj_biases)), 0, 1).astype(f32)
        bias_one = proj_biases[:, :, :hidden_size].reshape(-1)
        bias_two = proj_biases[:, :, hidden_size : 2 * hidden_size].reshape(-1)
        bias_three = proj_biases[:, :, 2 * hidden_size :].reshape(-1)

        bin_onehot = near_bins[:, None] == jnp.arange(time_table.shape[0], dtype=jnp.int32)[None, :]
        class_onehot = (
            near_labels[:, None] == jnp.arange(class_table.shape[0], dtype=jnp.int32)[None, :]
        )
        condition = jnp.dot(
            bin_onehot.astype(bf16), time_table, preferred_element_type=f32
        ) + jnp.dot(class_onehot.astype(bf16), class_table, preferred_element_type=f32)
        cond_act = jax.nn.silu(condition).astype(bf16)
        def near_rows(values):
            cut = values.reshape((-1, ROWS, image_count) + values.shape[1:])
            return cut.swapaxes(1, 2).reshape(values.shape)

        end_rows = [
            near_rows(values) for values in (cond_act, condition, bin_onehot, class_onehot)
        ]
        local_rows = w_ada.shape[1]
        wide_bias = lax.dynamic_update_slice(
            jnp.zeros((b_ada.shape[0], width), f32), b_ada, (0, me * local_rows)
        )
        partial_mods = (
            jnp.einsum("bd,tde->tbe", cond_act, w_ada, preferred_element_type=f32)
            + wide_bias[:, None, :]
        ).astype(bf16)
        mods = partial_mods.astype(f32)
        near_a = join(pair_a, arrived)
        row_a = swap_y(near_a)
        late = lax.all_gather(tie(shard_late, near_a), ("dp", "mp"), axis=0, tiled=False)
        proj_one = lax.all_gather(tie(w_first.T, near_a), ("dp", "mp"), axis=0, tiled=True)

        class Wide:
            def __init__(self, shard):
                self.value = shard
                self.left = list(far)
                self.arrived = swap(shard, self.left[0])

            def step(self):
                while len(self.left) > 1:
                    self.value = join(self.value, self.arrived)
                    self.left.pop(0)
                    self.arrived = swap(self.value, self.left[0])
                return self.value

            def end(self):
                return join(self.step(), self.arrived)

        wide_b = Wide(tie(jnp.concatenate((w_qkv[2:], w_out.T[None]), axis=0)[None], near_a))
        for mask in near_order[::-1]:
            half = mods.shape[1] // 2
            outgoing = mark(after(mods[:, half:]).astype(bf16))
            if mask == far[0]:
                pair_b = wide_b.step()
            mods = mods[:, :half] + after(swap(outgoing, mask)).astype(f32)
        modulation = after(mods)

        near_mods = jnp.stack((pick(modulation, side, 1), pick(modulation, 1 - side, 1)), axis=1)
        shift_one, scale_one = near_mods[0][:, None, :], near_mods[1][:, None, :]
        scale_own = scale_one[0]
        gate_one, shift_two, scale_two, gate_two = (near_mods[t][0:1] for t in range(2, 6))
        inputs = jnp.stack((pick(patches, side), pick(patches, 1 - side)), axis=0).astype(f32)

        near_b = wide_b.end()
        row_b = swap_y(near_b)
        wide_up = Wide(tie(w_up[None, None], pair_b))
        normed_one, inverse_one = layer_norm(inputs)
        act_one = mark((normed_one * (1.0 + scale_one) + shift_one).astype(bf16))
        last.extend(end_rows)

        def four(near, with_row):
            with_row = mark(after(with_row))
            return [near, with_row, swap_c(tie(near, with_row)), swap_c(with_row)]

        def dot(left, right, left_axis, right_axis):
            return lax.dot_general(
                left, right, (((left_axis,), (right_axis,)), ((), ())), preferred_element_type=f32
            )

        pieces_a = four(near_a, row_a)
        pair_up = wide_up.step()
        wide_down = Wide(tie(w_down.T[None, None], pair_up))
        (w_qk,) = gather_place(pieces_a, False, ((0, 2),))
        local_width = w_qk.shape[2]
        bias_query = flat_inner[:local_width]
        bias_value = flat_inner[local_width : 2 * local_width]
        bias_units = flat_inner[2 * local_width :]
        tokens = image_count * seq_len

        def flat(values):
            return values.reshape(tokens, values.shape[-1])

        act_flat = flat(act_one)
        qk_in = after(act_flat, w_qk)
        queries = (dot(qk_in, w_qk[0], 1, 0) + bias_query).astype(bf16)
        key_heads = dot(qk_in, w_qk[1], 1, 0).astype(bf16)
        mark(key_heads)
        pieces_b = four(near_b, row_b)
        near_up = wide_up.end()
        row_up = swap_y(near_up)
        w_value, full_out = gather_place(
            four(near_b, row_b), False, ((0, 1), (1, 2))
        )
        w_value, full_out = w_value[0], full_out[0]
        v_in = after(act_flat, w_value)
        val_heads = mark((dot(v_in, w_value, 1, 0) + bias_value).astype(bf16))
        wide_down.step()
        mixed_heads, log_total = attend(after(queries), key_heads, val_heads, seq_len)
        mixed_heads = mark(mixed_heads).reshape(image_count, seq_len, local_width)

        arrived = swap_x(mark(dot(after(mixed_heads[1]), full_out, 1, 1).astype(bf16)))
        attention = dot(after(mixed_heads[0]), full_out, 1, 1) + full_bout
        attention = mark(attention)
        near_down = wide_down.end()
        row_down = swap_y(near_down)
        pieces_up = four(near_up, row_up)
        attention = attention + after(arrived).astype(f32)
        first_sum = inputs[0] + gate_one * attention
        normed_two, inverse_two = layer_norm(first_sum)
        act_two = mark((normed_two * (1.0 + scale_two) + shift_two).astype(bf16))
        other_two = swap_x(act_two)
        (full_up,) = gather_place(pieces_up, False, ((0, 1),))
        full_up = mark(full_up[0])

        def feed(values):
            hidden = dot(after(values), full_up, 1, 0) + bias_units
            return hidden, mark(gelu_tanh(hidden).astype(bf16))

        hidden_own, active_own = feed(act_two)
        late_two = after(late)
        proj_two = mark(late_two[:, :hidden_size].reshape(dp * mp * hidden_size, -1))
        proj_three = mark(late_two[:, hidden_size:].reshape(dp * mp * b_third.shape[0], -1))
        hidden_other, active_other = feed(other_two)
        (full_down,) = gather_place(
            four(near_down, row_down), False, ((0, 1),)
        )
        full_down = mark(full_down[0])
        arrived = swap_x(mark(dot(after(active_other), full_down, 1, 1).astype(bf16)))
        branch = mark(dot(after(active_own), full_down, 1, 1))
        branch = branch + full_bdown + after(arrived).astype(f32)
        output = first_sum + gate_two * branch
        block_out = mark(output.astype(bf16))
        other_out = swap_x(block_out)

        target = pick(encoder_feats, side).astype(f32)
        pre_one = dot(after(block_out), proj_one, 1, 1) + bias_one
        act_pone = mark(jax.nn.silu(pre_one).astype(bf16))
        pre_two = dot(after(act_pone), proj_two, 1, 1) + bias_two
        act_ptwo = mark(jax.nn.silu(pre_two).astype(bf16))
        mapped = dot(after(act_ptwo), proj_three, 1, 1) + bias_three
        inv_map = lax.rsqrt(jnp.sum(mapped * mapped, axis=-1, keepdims=True) + epsilon)
        inv_target = lax.rsqrt(jnp.sum(target * target, axis=-1, keepdims=True) + epsilon)
        cosine = jnp.sum(mapped * target, axis=-1, keepdims=True) * inv_map * inv_target
        loss_weight = -0.5 * float(width)
        grad_mapped = mark(
            (
                loss_weight
                * (target * inv_map * inv_target - cosine * inv_map * inv_map * mapped)
            ).astype(bf16)
        )
        grad_bthird = jnp.sum(grad_mapped.astype(f32), axis=0, keepdims=True)
        three = Scatter([mark(dot(after(grad_mapped), act_ptwo, 0, 0).astype(bf16))], True)
        fly(other_out)
        land()
        three.send(1)
        grad_pre_two = mark(
            (dot(after(grad_mapped), proj_three, 1, 0) * silu_grad(pre_two)).astype(bf16)
        )
        grad_bsecond = jnp.sum(grad_pre_two.astype(f32), axis=0, keepdims=True)
        two = Scatter([mark(dot(after(grad_pre_two), act_pone, 0, 0).astype(bf16))], True)
        land()
        two.send(1)
        three.send(CORES)
        grad_pre_one = mark(
            (dot(after(grad_pre_two), proj_two, 1, 0) * silu_grad(pre_one)).astype(bf16)
        )
        grad_bfirst = jnp.sum(grad_pre_one.astype(f32), axis=0, keepdims=True)
        grad_feed = mark(dot(after(grad_pre_one), proj_one, 1, 0))

        grad_output = pick(cotangent, side).astype(f32) + grad_feed.astype(bf16).astype(f32)
        grad_branch = mark((gate_two * grad_output).astype(bf16))
        grad_gate_two = jnp.sum(grad_output * branch, axis=0, keepdims=True)
        grad_bdown = jnp.sum(grad_branch.astype(f32), axis=0, keepdims=True)
        land()
        other_branch = fly(swap_x(grad_branch))
        two.send(CORES, 0, 2)
        early_two = hold()
        one = Scatter([mark(dot(after(grad_pre_one), block_out, 0, 0).astype(bf16))], True)

        def feed_back(incoming, hidden):
            grad_active = dot(after(incoming), full_down, 1, 0)
            return mark((grad_active * gelu_grad(hidden)).astype(bf16))

        hidden_grad_own = feed_back(grad_branch, hidden_own)
        land()
        three.send(0)
        one.send(1)
        hidden_grad_other = feed_back(other_branch, hidden_other)
        outgoing = mark(dot(after(hidden_grad_other), full_up, 1, 1).astype(bf16))
        land()
        arrived = fly(swap_x(outgoing))
        three.send(far[-1])
        two.send(CORES, 1, 2)
        slow = hold()
        fly(early_two)
        grad_act_two = mark(dot(after(hidden_grad_own), full_up, 1, 1))
        grad_bunits = jnp.sum(hidden_grad_own.astype(f32), axis=0, keepdims=True) + jnp.sum(
            hidden_grad_other.astype(f32), axis=0, keepdims=True
        )
        branch_both = jnp.concatenate((grad_branch, other_branch), axis=0)
        active_both = jnp.concatenate((active_own, active_other), axis=0)
        grad_wdown = mark(dot(after(branch_both), active_both, 0, 0).astype(bf16))
        own_down = lax.psum_scatter(grad_wdown, "dp", scatter_dimension=0, tiled=True)
        land()
        for mask in far[-2::-1]:
            three.send(mask)
        grad_act_two = after(grad_act_two) + arrived.astype(f32)
        grad_shift_two = jnp.sum(grad_act_two, axis=0, keepdims=True)
        grad_scale_two = jnp.sum(grad_act_two * normed_two, axis=0, keepdims=True)
        grad_first_sum = grad_output + norm_back(
            grad_act_two * (1.0 + scale_two), normed_two, inverse_two
        )

        grad_attention = mark((gate_one * grad_first_sum).astype(bf16))
        grad_gate_one = jnp.sum(grad_first_sum * attention, axis=0, keepdims=True)
        grad_bout = jnp.sum(grad_attention.astype(f32), axis=0, keepdims=True)
        late_two = slow
        land()
        other_attention = fly(swap_x(grad_attention))
        one.send(CORES)
        slow = hold()
        act_both = jnp.concatenate((act_two, other_two), axis=0)
        hidden_both = jnp.concatenate((hidden_grad_own, hidden_grad_other), axis=0)
        grad_wup = mark(dot(after(act_both), hidden_both, 0, 0).astype(bf16))
        own_up = lax.psum_scatter(grad_wup, "dp", scatter_dimension=0, tiled=True)
        fly(late_two)
        land()
        two.send(0)
        slower = hold()
        attention_both = mark(
            jnp.concatenate((after(grad_attention), other_attention), axis=0)
        )
        grad_mixed = mark(dot(after(attention_both), full_out, 1, 0).astype(bf16))
        my_core = core[None].astype(jnp.int32)
        halves = split_grads(
            after(attention_both), flat(mixed_heads)[None], my_core, planes * ROWS
        )
        out = Scatter.from_halves(halves[0], mark(halves[1]))
        land()
        grad_three = mark(
            attend_back(queries, key_heads, val_heads, log_total, after(grad_mixed), seq_len)
        )
        grad_bquery = jnp.sum(grad_three[0].astype(f32), axis=0, keepdims=True)
        grad_bvalue = jnp.sum(grad_three[2].astype(f32), axis=0, keepdims=True)
        fly(slow)
        fly(slower)
        land()
        one.send(0)
        out.send(CORES)
        two.send(far[-1])

        def part_one(start):
            held = after(grad_three)
            return sum(
                dot(held[t, start : start + seq_len], weight, 1, 1)
                for t, weight in enumerate((w_qk[0], w_qk[1], w_value))
            )

        outgoing = mark(part_one(seq_len).astype(bf16))
        grad_act_one = mark(part_one(0))
        arrived = fly(swap_x(outgoing))
        halves = split_grads(act_flat, after(grad_three), my_core, planes * ROWS)
        qkv = Scatter.from_halves(halves[0], mark(halves[1]))
        land()
        for mask in far[-2::-1]:
            two.send(mask)
        one.send(far[-1])
        out.send(far[-1])
        normed_own, inverse_own = normed_one[0], inverse_one[0]
        grad_act_one = after(grad_act_one) + arrived.astype(f32)
        grad_shift_one = jnp.sum(grad_act_one, axis=0, keepdims=True)
        grad_scale_one = jnp.sum(grad_act_one * normed_own, axis=0, keepdims=True)
        grad_own = grad_first_sum + norm_back(
            grad_act_one * (1.0 + scale_own), normed_own, inverse_own
        )
        sent = [
            grad_shift_one,
            grad_scale_one,
            grad_gate_one,
            grad_shift_two,
            grad_scale_two,
            grad_gate_two,
            grad_bout,
            grad_bdown,
            grad_bfirst,
            grad_bsecond,
            grad_bthird,
            grad_bquery,
            grad_bvalue,
            grad_bunits,
        ]
        starts = [0]
        for piece in sent:
            starts.append(starts[-1] + piece.shape[1])
        sent = jnp.concatenate([piece.astype(bf16) for piece in sent], axis=1)
        mark(sent)
        row_sent = swap(sent, near_order[0])
        qkv.send(CORES)
        near_sent = mark(jnp.concatenate((sent, after(row_sent)), axis=0))
        side_sent = swap_x(near_sent)
        grad_other = swap_x(tie(grad_own.astype(bf16), near_sent))
        near_sent = mark(ordered(near_sent, after(side_sent)).reshape(-1, sent.shape[1]))
        for k, mask in enumerate(near_order[1:]):
            arrived = swap(near_sent, mask)
            near_sent = mark(jnp.concatenate((near_sent, after(arrived)), axis=0))
            if k == 0:
                land()
                qkv.send(far[-1])
        land()
        for mask in far[-2::-1]:
            qkv.send(mask)
            one.send(mask)
            out.send(mask)
        near_sent = after(near_sent)
        def own_part(index, count, parts, values):
            held = values[:, starts[index] : starts[index] + count * parts]
            at = me if parts == dp else me * mp + side
            return lax.dynamic_slice_in_dim(held, at * count, count, 1)

        totals = jnp.sum(near_sent.astype(f32), axis=0, keepdims=True)
        same_side = jnp.arange(near_sent.shape[0]) // ROWS % image_count == side
        inner_total = jnp.sum(
            jnp.where(same_side[:, None], near_sent[:, starts[11] :].astype(f32), 0.0),
            axis=0,
            keepdims=True,
        )
        sum_bada = jnp.concatenate([own_part(t, thin, dp, totals) for t in range(6)], axis=0)
        sum_bout = own_part(6, thin, dp, totals)[0]
        sum_bdown = own_part(7, thin, dp, totals)[0]
        sum_bfirst = own_part(8, hidden_size, dp * mp, totals)[0]
        sum_bsecond = own_part(9, hidden_size, dp * mp, totals)[0]
        sum_bthird = own_part(10, b_third.shape[0], dp * mp, totals)[0]
        sum_inner = lax.dynamic_slice_in_dim(inner_total, me * inner_size, inner_size, 1)
        cond_act, condition, bin_onehot, class_onehot = end_rows
        every_mods = [near_sent[:, starts[t] : starts[t + 1]] for t in range(6)]
        sum_wada = jnp.stack([dot(cond_act, mods, 0, 0) for mods in every_mods], axis=0)
        grad_cond = sum(dot(mods, w_ada[t], 1, 1) for t, mods in enumerate(every_mods))
        grad_cond = grad_cond * silu_grad(condition)
        mark(sum_wada)
        sum_time = jnp.einsum(
            "bn,bd->nd", bin_onehot.astype(f32), grad_cond, precision=lax.Precision.HIGHEST
        )
        sum_class = jnp.einsum(
            "bn,bd->nd", class_onehot.astype(f32), grad_cond, precision=lax.Precision.HIGHEST
        )

        (sum_wfirst,) = one.finish()
        sum_down = after(own_down).astype(f32)
        sum_up = after(own_up).astype(f32)
        (sum_wsecond,) = two.finish()
        (sum_wthird,) = three.finish()
        sum_attn = qkv.finish() + out.finish()
        return (
            ordered(block_out, tie(other_out, sum_wada)),
            ordered(grad_own, grad_other.astype(f32)),
            jnp.stack(sum_attn[:3], axis=0),
            sum_attn[3].T,
            sum_up,
            sum_down.T,
            sum_wada,
            sum_time,
            sum_class,
            sum_inner,
            sum_bout,
            sum_bdown,
            sum_bada,
            sum_wfirst.T,
            sum_wsecond.T,
            sum_wthird.T,
            sum_bfirst,
            sum_bsecond,
            sum_bthird,
        )

    placed = (
        P("dp", None, None),
        P("dp"),
        P("dp"),
        P("dp", None, None),
        P("dp", None, None),
        P(None, "dp", "mp"),
        P("mp", "dp"),
        P("dp", "mp"),
        P("mp", "dp"),
        P(None, "dp", None),
        P(None, "dp"),
        P(None, "dp"),
        P("mp", "dp"),
        P("dp"),
        P("dp"),
        P(None, "dp"),
        P(None, ("dp", "mp")),
        P(None, ("dp", "mp")),
        P(None, ("dp", "mp")),
        P(("dp", "mp")),
        P(("dp", "mp")),
        P(("dp", "mp")),
    )
    return jax.shard_map(
        shards,
        mesh=mesh,
        in_specs=placed,
        out_specs=(
            P("dp", None, None),
            P("dp", None, None),
            P(None, "dp", "mp"),
            P("mp", "dp"),
            P("dp", "mp"),
            P("mp", "dp"),
            P(None, "dp", None),
            P(None, "dp"),
            P(None, "dp"),
            P("mp", "dp"),
            P("dp"),
            P("dp"),
            P(None, "dp"),
            P(None, ("dp", "mp")),
            P(None, ("dp", "mp")),
            P(None, ("dp", "mp")),
            P(("dp", "mp")),
            P(("dp", "mp")),
            P(("dp", "mp")),
        ),
        check_vma=False,
    )
```
